512 devices in a mesh: seq: 64 (over z_lo, x, core), head: 8 (over y, z_hi).
Axes of the slice: x: 4, y: 4, z: 16 (z_hi: 2, z_lo: 8; z = z_hi * 8 + z_lo), core: 2. Of those that a mesh axis runs over, the one named last changes fastest.
Arguments:
- layer_input: bfloat16 [8192, 8192], P('seq', 'head'), may hold values from -6 to 6
- queries: bfloat16 [8192, 4096], P('seq', 'head'), may hold values from -32 to 32
- key_states: bfloat16 [8192, 1024], P('seq', 'head'), may hold values from -32 to 32
- value_states: bfloat16 [8192, 1024], P('seq', 'head'), may hold values from -6 to 6
- out_grad: bfloat16 [8192, 4096], P('seq', 'head'), may hold values from -24 to 24
- input_hash: int32 [2, 8192], P(None, 'head'), may hold values from 0 to 63
- query_hash: int32 [2, 4096], P(None, 'head'), may hold values from 0 to 63
- key_hash: int32 [2, 1024], P(None, 'head'), may hold values from 0 to 63
- value_hash: int32 [2, 1024], P(None, 'head'), may hold values from 0 to 63
- doc_starts: int32 [64], replicated, may hold values from 0 to 8128, as said below
- doc_rows: int32 [64], replicated, may hold values from 0 to 63, each once
Outputs:
- sketches: float32 [64, 3, 4096], P('seq', None, 'head')
The draws below stay inside these ranges and needn't reach their ends.
Inputs may be any that keep to these rules, and one draw needn't show every extreme that they name: `input_hash`: row 0 holds each input feature's bucket; row 1 its sign: +1 where even, -1 where odd. `query_hash`: row 0 holds each query feature's bucket; row 1 its sign: +1 where even, -1 where odd. `key_hash`: row 0 holds each key feature's bucket; row 1 its sign: +1 where even, -1 where odd. `value_hash`: row 0 holds each value feature's bucket; row 1 its sign: +1 where even, -1 where odd. `doc_starts`: increasing; the first is 0; a document starts at every multiple of 512; every document holds 64 to 320 tokens, both reached, so the 128 tokens of one device touch at most 3 documents, and some device's touch 3. `doc_rows`: each output row receives exactly one document.
All inputs are finite; a program needn't handle non-finite values.
Results may differ from the reference program's by a relative error of at most 0.015.
Values may be sent and summed in bfloat16 or wider, within the bound.
A program may use at most 64 MiB of HBM per device.

```python
import math
import jax
import jax.numpy as jnp
from jax import lax

D = 8192
HEAD_DIM = 128
QH_DEV = 4
SK = 64
TOK_DEV = 128
TOKENS = 8192
QDIM = 4096
KVDIM = 1024
DOCS = 64
MIN_LEN = 64


def draw_queries(key, part):
    key = jax.random.fold_in(key, 7)
    return jnp.clip(jax.random.normal(key, (TOKENS, QDIM), jnp.float32), -6.0, 6.0).astype(jnp.bfloat16)


def draw_key_states(key, part):
    key = jax.random.fold_in(key, 5)
    return jnp.clip(jax.random.normal(key, (TOKENS, KVDIM), jnp.float32), -6.0, 6.0).astype(jnp.bfloat16)


def draw_doc_starts(key, part):
    key = jax.random.fold_in(key, 11)
    group_count = DOCS // 4
    extra_room = 2 * TOK_DEV
    cuts = jnp.sort(jax.random.randint(jax.random.fold_in(key, 1), (group_count, 3), 0, extra_room + 1), axis=1)
    chosen = jax.random.randint(jax.random.fold_in(key, 2), (2,), 0, group_count)
    first_forced = chosen[0]
    second_forced = jnp.mod(first_forced + 1 + jnp.mod(chosen[1], group_count - 1), group_count)
    cuts = cuts.at[first_forced].set(jnp.full((3,), TOK_DEV // 8, jnp.int32))
    cuts = cuts.at[second_forced].set(jnp.zeros((3,), jnp.int32))
    cuts = cuts.at[group_count - 1, 2].set(extra_room)
    inner = jnp.concatenate([jnp.zeros((group_count, 1), jnp.int32), jnp.arange(1, 4, dtype=jnp.int32)[None, :] * MIN_LEN + cuts], axis=1)
    group_firsts = jnp.arange(group_count, dtype=jnp.int32)[:, None] * (4 * TOK_DEV)
    return (group_firsts + inner).reshape(DOCS).astype(jnp.int32)


def set_ends(result, stream_key, smallest, high):
    place = [jax.random.randint(jax.random.fold_in(stream_key, axis), (), 0, length) for axis, length in enumerate(result.shape)]
    widest = result.shape.index(max(result.shape))
    neighbour = place[:widest] + [(place[widest] + 1) % result.shape[widest]] + place[widest + 1:]
    return result.at[tuple(place)].set(smallest).at[tuple(neighbour)].set(high)


def block_scale(rng, dims, split, smallest, top_value):
    def one(dim, parts):
        draws = jax.random.uniform(jax.random.fold_in(jax.random.fold_in(rng, 6), dim), (parts,), jnp.float32, smallest / len(split), top_value / len(split))
        return jnp.repeat(jnp.exp(draws), dims[dim] // parts).reshape((-1,) + (1,) * (len(dims) - dim - 1))

    factor_of = one(*split[0])
    for cut in split[1:]:
        factor_of = factor_of * one(*cut)
    return factor_of


def bell_draw(rng, dims, scale, limit, cuts=(), kind=jnp.bfloat16):
    factor_of = block_scale(rng, dims, cuts, -0.22, 0.18) if cuts else 1.0
    result = jax.random.normal(rng, dims, jnp.float32) * scale * factor_of
    return jnp.minimum(jnp.maximum(result, -limit), limit).astype(kind)


def setup_inputs(seed: int = 0) -> dict:
    seeds = jax.random.split(jax.random.key(seed), 12)
    layer_input = bell_draw(seeds[0], (TOKENS, D), 1.0, 6.0, ((0, 64), (1, 8)))
    queries = draw_queries(jax.random.fold_in(seeds[11], 71), 0)
    key_states = draw_key_states(jax.random.fold_in(seeds[11], 71), 0)
    value_states = bell_draw(seeds[3], (TOKENS, KVDIM), 1.0, 6.0, ((0, 64), (1, 8)))
    out_grad = bell_draw(seeds[4], (TOKENS, QDIM), 4.0, 24.0, ((0, 64), (1, 8)))
    input_hash = set_ends(jax.random.randint(seeds[5], (2, D), 0, SK), jax.random.fold_in(seeds[5], 1), 0, SK - 1).astype(jnp.int32)
    query_hash = set_ends(jax.random.randint(seeds[6], (2, QDIM), 0, SK), jax.random.fold_in(seeds[6], 1), 0, SK - 1).astype(jnp.int32)
    key_hash = set_ends(jax.random.randint(seeds[7], (2, KVDIM), 0, SK), jax.random.fold_in(seeds[7], 1), 0, SK - 1).astype(jnp.int32)
    value_hash = set_ends(jax.random.randint(seeds[8], (2, KVDIM), 0, SK), jax.random.fold_in(seeds[8], 1), 0, SK - 1).astype(jnp.int32)
    doc_starts = draw_doc_starts(jax.random.fold_in(seeds[11], 71), 0)
    doc_rows = jax.random.permutation(seeds[10], DOCS).astype(jnp.int32)
    return dict(layer_input=layer_input, queries=queries, key_states=key_states, value_states=value_states, out_grad=out_grad, input_hash=input_hash, query_hash=query_hash, key_hash=key_hash, value_hash=value_hash, doc_starts=doc_starts, doc_rows=doc_rows)


masked_score = -1e+30
highest = lax.Precision.HIGHEST

def rounded(values):
    return lax.optimization_barrier(values.astype(jnp.bfloat16)).astype(jnp.float32)

def signed_table(hashes, buckets_count):
    matches = hashes[0][:, None] == jnp.arange(buckets_count, dtype=jnp.int32)[None, :]
    sign_values = 1.0 - 2.0 * (hashes[1] % 2).astype(jnp.float32)
    return jnp.where(matches, sign_values[:, None], 0.0)

def sketch_rows(rows_in, hashes):
    sign_table = signed_table(hashes, SK)
    factor = math.sqrt(SK / rows_in.shape[1])
    return jnp.dot(rows_in.astype(jnp.float32), sign_table, precision=highest) * factor

def group_grads(group_queries, group_keys, group_values, group_out_grads):
    score_scale = 1.0 / math.sqrt(HEAD_DIM)
    key_float = group_keys.astype(jnp.float32)
    value_float = group_values.astype(jnp.float32)
    key_places = jnp.arange(TOKENS, dtype=jnp.int32)
    block_rows = math.gcd(TOKENS, 256)
    block_count = TOKENS // block_rows

    def one_block(iteration_state, block_index):
        key_sum, value_sum = iteration_state
        first_row = block_index * block_rows
        query_block = lax.dynamic_slice_in_dim(group_queries, first_row, block_rows, 0).astype(jnp.float32)
        grad_block = lax.dynamic_slice_in_dim(group_out_grads, first_row, block_rows, 0).astype(jnp.float32)
        query_places = first_row + jnp.arange(block_rows, dtype=jnp.int32)
        causal = key_places[None, None, :] <= query_places[:, None, None]
        scores = jnp.einsum('thd,ud->thu', query_block, key_float, precision=highest) * score_scale
        scores = jnp.where(causal, scores, masked_score)
        row_top = lax.optimization_barrier(jnp.max(scores, axis=-1, keepdims=True))
        log_total = row_top + jnp.log(lax.optimization_barrier(jnp.sum(jnp.exp(scores - row_top), axis=-1, keepdims=True)))
        weights = jnp.where(causal, jnp.exp(scores - log_total), 0.0)
        weights_low = rounded(weights)
        attended = jnp.einsum('thu,ud->thd', weights_low, value_float, precision=highest)
        row_delta = lax.optimization_barrier(jnp.sum(grad_block * attended, axis=-1, keepdims=True))
        weight_grads = jnp.einsum('thd,ud->thu', grad_block, value_float, precision=highest)
        score_grads = rounded(weights * (weight_grads - row_delta))
        query_grads = jnp.einsum('thu,ud->thd', score_grads, key_float, precision=highest) * score_scale
        key_sum = key_sum + jnp.einsum('thu,thd->ud', score_grads, query_block, precision=highest)
        value_sum = value_sum + jnp.einsum('thu,thd->ud', weights_low, grad_block, precision=highest)
        return ((key_sum, value_sum), query_grads.astype(jnp.bfloat16))
    zero_rows = jnp.zeros((TOKENS, HEAD_DIM), jnp.float32)
    sums, query_grads = lax.scan(one_block, (zero_rows, zero_rows), jnp.arange(block_count, dtype=jnp.int32))
    key_sum, value_sum = sums
    query_grads = query_grads.reshape(TOKENS, QH_DEV, HEAD_DIM)
    return (query_grads, (key_sum * score_scale).astype(jnp.bfloat16), value_sum.astype(jnp.bfloat16))

def reference(layer_input, queries, key_states, value_states, out_grad, input_hash, query_hash, key_hash, value_hash, doc_starts, doc_rows):
    kv_groups = KVDIM // HEAD_DIM
    grouped_queries = queries.reshape(TOKENS, kv_groups, QH_DEV, HEAD_DIM).transpose(1, 0, 2, 3)
    grouped_grads = out_grad.reshape(TOKENS, kv_groups, QH_DEV, HEAD_DIM).transpose(1, 0, 2, 3)
    grouped_keys = key_states.reshape(TOKENS, kv_groups, HEAD_DIM).transpose(1, 0, 2)
    grouped_values = value_states.reshape(TOKENS, kv_groups, HEAD_DIM).transpose(1, 0, 2)
    query_grads, key_grads, value_grads = lax.map(lambda operands: group_grads(*operands), (grouped_queries, grouped_keys, grouped_values, grouped_grads))
    query_grads = query_grads.transpose(1, 0, 2, 3).reshape(TOKENS, QDIM)
    key_grads = key_grads.transpose(1, 0, 2).reshape(TOKENS, KVDIM)
    value_grads = value_grads.transpose(1, 0, 2).reshape(TOKENS, KVDIM)
    input_sketch = sketch_rows(layer_input, input_hash)
    grad_sketches = jnp.stack([sketch_rows(query_grads, query_hash), sketch_rows(key_grads, key_hash), sketch_rows(value_grads, value_hash)])
    places = jnp.arange(TOKENS, dtype=jnp.int32)
    doc_of = lax.optimization_barrier(jnp.sum((doc_starts[None, :] <= places[:, None]).astype(jnp.int32), axis=1)) - 1
    doc_hot = (doc_of[:, None] == jnp.arange(DOCS, dtype=jnp.int32)[None, :]).astype(jnp.float32)
    per_doc = jnp.einsum('td,ta,ptb->pdab', doc_hot, input_sketch, grad_sketches, precision=highest)
    per_doc = per_doc.transpose(1, 0, 2, 3).reshape(DOCS, 3, SK * SK)
    return jnp.zeros((DOCS, 3, SK * SK), jnp.float32).at[doc_rows].set(per_doc)
```

```python
import functools
import math

import jax
import jax.numpy as jnp
from jax import lax
from jax.experimental import pallas as pl
from jax.experimental.pallas import tpu as pltpu
from jax.sharding import PartitionSpec as P

SEQ_GRID = (8, 4, 2)
HEAD_GRID = (4, 2)

T = 128
F = 128
H = 4
SK = 64
GROUP = 4
DOCS_MOST = 8
LOW = -1e30
MESH = pl.DeviceIdType.MESH
F32 = jnp.float32
BF16 = jnp.bfloat16


def dot_nt(a, b):
    return lax.dot_general(a, b, (((1,), (1,)), ((), ())), preferred_element_type=F32)


def dot_nn(a, b):
    return jnp.dot(a, b, preferred_element_type=F32)


def sign_table(hashes):
    buckets = lax.broadcasted_iota(jnp.int32, (SK, hashes.shape[1]), 0)
    signs = (1 - 2 * (hashes[1:2, :] & 1)).astype(F32)
    return jnp.where(buckets == hashes[0:1, :], signs, 0.0).astype(BF16)


def rem(value, count):
    return lax.rem(value + count, count)


class Place:
    def __init__(self):
        self.planes, self.chips, self.cores = SEQ_GRID
        self.ys, self.halves = HEAD_GRID
        self.width = self.chips * self.cores
        seq = lax.axis_index("seq")
        head = lax.axis_index("head")
        self.seq, self.head = seq, head
        self.i = lax.rem(seq, self.width)
        self.z = seq // self.width
        self.c = lax.rem(self.i, self.cores)
        self.x = self.i // self.cores
        self.y = head // self.halves
        self.half = lax.rem(head, self.halves)

    def at(self, z=None, i=None, y=None, half=None):
        z = self.z if z is None else z
        i = self.i if i is None else i
        y = self.y if y is None else y
        half = self.half if half is None else half
        return (z * self.width + i, y * self.halves + half)


def remote(src, dst, send_sem, recv_sem, device):
    return pltpu.make_async_remote_copy(
        src_ref=src, dst_ref=dst, send_sem=send_sem, recv_sem=recv_sem, device_id=device, device_id_type=MESH
    )


def meet(devices):
    barrier = pltpu.get_barrier_semaphore()
    for device in devices:
        pl.semaphore_signal(barrier, inc=1, device_id=device, device_id_type=MESH)
    pl.semaphore_wait(barrier, len(devices))


def attention_kernel(
    x_ref, q_ref, k_ref, v_ref, do_ref, xh_ref, qh_ref, kh_ref, vh_ref,
    input_out, grad_out,
    qall, kv, scores, wgrads, stat, kmt, stat_send, stat_recv, fin, total, dq_acc, dkv_acc,
    dkv_send, dkv_recv, dq_send, dq_recv, iy, iz,
    q_recv, q_own, q_ring, q_sib, kv_send_sem, kv_recv_sem, st_send_sem, st_recv_sem, fin_send_sem, fin_recv_sem,
    dkv_send_sem, dkv_recv_sem, dq_send_sem, dq_recv_sem, iy_send_sem, iy_recv_sem, iz_send_sem, iz_recv_sem,
):
    me = Place()
    planes, chips, width = me.planes, me.chips, me.width
    x, c, z, i = me.x, me.c, me.z, me.i
    rows = 2 * T
    scale = 1.0 / math.sqrt(F)
    scale2 = scale * math.log2(math.e)

    mine = pl.ds(pl.multiple_of(c * T, T), T)
    other = pl.ds(pl.multiple_of((1 - c) * T, T), T)
    for h in range(H):
        qall[x, 0, h, mine, :] = q_ref[:, h * F:(h + 1) * F]
        qall[x, 1, h, mine, :] = do_ref[:, h * F:(h + 1) * F]
    kv[z, 0] = k_ref[...]
    kv[z, 1] = v_ref[...]

    peers = [me.at(i=rem(i + o, width)) for o in range(1, width)]
    friends = peers + [me.at(z=rem(z + o, planes)) for o in range(1, planes)]
    friends += [me.at(y=rem(me.y + o, me.ys)) for o in range(1, me.ys)]
    friends += [me.at(half=1 - me.half)] if me.halves > 1 else []
    meet(friends)

    def piece(step, core, part):
        s = rem(x + step, chips)
        ref = qall.at[s, part, :, pl.ds(pl.multiple_of(core * T, T), T), :]
        return ref, q_recv.at[s, core, part]

    def send_piece(step, core, part, send_sem, target):
        ref, recv_sem = piece(step, core, part)
        return remote(ref, ref, send_sem, recv_sem, target)

    sibling = me.at(i=x * 2 + 1 - c)
    right = me.at(i=rem(x + 1, chips) * 2 + c)
    left = me.at(i=rem(x + chips - 1, chips) * 2 + c)
    own_copies = [
        send_piece(0, c, part, q_own.at[n, part], target)
        for n, target in enumerate((sibling, right, left)) for part in range(2)
    ]
    ring_copies = [
        send_piece(chips - 1, c, 0, q_ring.at[0], right),
        send_piece(1, c, 1, q_ring.at[1], left),
    ]
    sib_copies = {
        (step, part): send_piece(step, c, part, q_sib.at[step - 1, part], sibling)
        for step in (1, 2, 3) for part in range(2)
    }

    def wait_piece(step, core, part):
        ref, recv_sem = piece(step, core, part)
        remote(ref, ref, q_own.at[0, 0], recv_sem, sibling).wait_recv()

    def kv_copy(b):
        return remote(kv.at[b], kv.at[b], kv_send_sem.at[b], kv_recv_sem.at[b], me.at(z=rem(z + 1, planes)))

    has_above = z < planes - 1

    @pl.when(has_above)
    def _():
        kv_copy(z).start()

    for copy in own_copies:
        copy.start()

    input_part = dot_nt(sign_table(xh_ref[...]), x_ref[...])
    iy[me.y] = input_part.astype(BF16)
    iy_copies = [
        remote(iy.at[me.y], iy.at[me.y], iy_send_sem.at[o - 1], iy_recv_sem.at[me.y], me.at(y=rem(me.y + o, me.ys)))
        for o in range(1, me.ys)
    ]
    for copy in iy_copies:
        copy.start()
    iz_copy = remote(iz.at[me.half], iz.at[me.half], iz_send_sem.at[0], iz_recv_sem.at[me.half], me.at(half=1 - me.half))

    def input_over_y():
        for o in range(1, me.ys):
            y = rem(me.y + o, me.ys)
            remote(iy.at[y], iy.at[y], iy_send_sem.at[0], iy_recv_sem.at[y], me.at(y=y)).wait_recv()
        summed = iy[0].astype(F32)
        for y in range(1, me.ys):
            summed = summed + iy[y].astype(F32)
        iz[me.half] = summed.astype(BF16)
        if me.halves > 1:
            iz_copy.start()

    query_table = sign_table(qh_ref[...])
    query_tables = jnp.concatenate([query_table[:, h * F:(h + 1) * F] for h in range(H)], axis=0)
    key_table = sign_table(kh_ref[...])
    value_table = sign_table(vh_ref[...])

    for s in range(chips):
        stat[s, 0:1, :] = jnp.full((1, H * rows), LOW, F32)
        stat[s, 1:3, :] = jnp.zeros((2, H * rows), F32)

    def first_unit(s, k, masked):
        b = z - k
        for h in range(H):
            cols = pl.ds(h * rows, rows)
            st = dot_nt(kv[b, 0], qall[s, 0, h]) * scale2
            if masked:
                key_place = lax.broadcasted_iota(jnp.int32, (T, rows), 0) + i * T
                query_place = lax.broadcasted_iota(jnp.int32, (T, rows), 1) + s * rows
                st = jnp.where(key_place <= query_place, st, LOW)
            dp = dot_nt(kv[b, 1], qall[s, 1, h])
            scores[s, k, :, cols] = st
            wgrads[s, k, :, cols] = dp
            old_top = stat[s, 0:1, cols]
            top = jnp.maximum(old_top, jnp.max(st, axis=0, keepdims=True))
            e = jnp.exp2(st - top)
            keep = jnp.exp2(old_top - top)
            stat[s, 0:1, cols] = top
            stat[s, 1:2, cols] = stat[s, 1:2, cols] * keep + jnp.sum(e, axis=0, keepdims=True)
            stat[s, 2:3, cols] = stat[s, 2:3, cols] * keep + jnp.sum(e * dp, axis=0, keepdims=True)

    def first_step(t, carry):
        @pl.when(jnp.logical_and(t >= 1, t <= z))
        def _():
            kv_copy(z - t).wait_recv()

            @pl.when(has_above)
            def _():
                kv_copy(z - t).start()

        @pl.when(t <= z)
        def _():
            kmt[t] = dot_nt(query_tables, kv[z - t, 0]).astype(BF16)

        @pl.when(t == 0)
        def _():
            for part in range(2):
                wait_piece(0, 1 - c, part)

        @pl.when(t == 2)
        def _():
            for step in (chips - 1, 1):
                for part in range(2):
                    wait_piece(step, c, part)
                    sib_copies[(step, part)].start()
                ring_copies[0 if step == chips - 1 else 1].start()

        @pl.when(t == 3)
        def _():
            for step in (chips - 1, 1):
                for part in range(2):
                    wait_piece(step, 1 - c, part)
            input_over_y()

        @pl.when(t == 5)
        def _():
            for part in range(2):
                wait_piece(2, c, part)
                sib_copies[(2, part)].start()

        @pl.when(t == 6)
        def _():
            for part in range(2):
                wait_piece(2, 1 - c, part)

        def over_chips(r, carry):
            s = rem(x + r * (r + 1) // 2, chips)
            active = 3 * ((r + 1) // 2)
            low = jnp.where(t == active, 0, t)
            high = jnp.where(t >= active, jnp.minimum(t, z) + 1, 0)

            @pl.when(jnp.logical_and(low == 0, high > 0))
            def _():
                first_unit(s, 0, True)

            def over_blocks(k, carry):
                first_unit(s, k, False)
                return carry

            return lax.fori_loop(jnp.maximum(low, 1), high, over_blocks, carry)

        return lax.fori_loop(0, chips, over_chips, carry)

    lax.fori_loop(0, 8, first_step, 0)

    for s in range(chips):
        for core in range(2):
            for h in range(H):
                first = h * rows + core * T
                stat_send[s * 2 + core, 0:3, h * T:(h + 1) * T] = stat[s, 0:3, first:first + T]
    st_copies = [
        remote(
            stat_send.at[rem(i + o, width)], stat_recv.at[i], st_send_sem.at[o - 1], st_recv_sem.at[i],
            me.at(i=rem(i + o, width)),
        )
        for o in range(1, width)
    ]
    for copy in st_copies:
        copy.start()
    stat_recv[i] = stat_send[i]
    for o in range(1, width):
        p = rem(i + o, width)
        remote(stat_send.at[p], stat_recv.at[p], st_send_sem.at[0], st_recv_sem.at[p], me.at(i=p)).wait_recv()
    top = stat_recv[0, 0:1, :]
    for p in range(1, width):
        top = jnp.maximum(top, stat_recv[p, 0:1, :])
    weight_sum = jnp.zeros_like(top)
    delta_sum = jnp.zeros_like(top)
    for p in range(width):
        factor = jnp.exp2(stat_recv[p, 0:1, :] - top)
        weight_sum = weight_sum + stat_recv[p, 1:2, :] * factor
        delta_sum = delta_sum + stat_recv[p, 2:3, :] * factor
    fin[i, 0:1, :] = top + jnp.log2(weight_sum)
    fin[i, 1:2, :] = delta_sum / weight_sum
    fin_copies = [
        remote(fin.at[i], fin.at[i], fin_send_sem.at[o - 1], fin_recv_sem.at[i], me.at(i=rem(i + o, width)))
        for o in range(1, width)
    ]
    for copy in fin_copies:
        copy.start()
    dq_acc[...] = jnp.zeros_like(dq_acc)
    for o in range(1, width):
        p = rem(i + o, width)
        remote(fin.at[p], fin.at[p], fin_send_sem.at[0], fin_recv_sem.at[p], me.at(i=p)).wait_recv()
    for s in range(chips):
        for core in range(2):
            for h in range(H):
                first = h * rows + core * T
                total[s, 0:2, first:first + T] = fin[s * 2 + core, 0:2, h * T:(h + 1) * T]

    def second_unit(s, k):
        lows, grads = [], []
        for h in range(H):
            cols = pl.ds(h * rows, rows)
            p = jnp.exp2(scores[s, k, :, cols] - total[s, 0:1, cols])
            g = p * (wgrads[s, k, :, cols] - total[s, 1:2, cols])
            lows.append(p.astype(BF16))
            g = g.astype(BF16)
            grads.append(g)
            dq_acc[s] += dot_nn(kmt[k, h * SK:(h + 1) * SK, :], g)
        low = jnp.concatenate(lows, axis=1)
        grad = jnp.concatenate(grads, axis=1)
        dkv_acc[0] += dot_nn(grad, qall[s, 0].reshape(H * rows, F))
        dkv_acc[1] += dot_nn(low, qall[s, 1].reshape(H * rows, F))

    def dkv_copy(k, b):
        return remote(dkv_send.at[k], dkv_recv.at[z], dkv_send_sem.at[k], dkv_recv_sem.at[z], me.at(z=b))

    def second_step(n, carry):
        k = z - n
        dkv_acc[...] = jnp.zeros_like(dkv_acc)

        def over_chips(s, carry):
            second_unit(s, k)
            return carry

        lax.fori_loop(0, chips, over_chips, 0)
        dkv_send[k, 0:SK, :] = dot_nt(key_table, (dkv_acc[0] * scale).astype(BF16)).astype(BF16)
        dkv_send[k, SK:, :] = dot_nt(value_table, dkv_acc[1].astype(BF16)).astype(BF16)

        @pl.when(k > 0)
        def _():
            dkv_copy(k, n).start()

        return carry

    lax.fori_loop(0, z + 1, second_step, 0)

    for s in range(chips):
        for core in range(2):
            dq_send[s * 2 + core] = (dq_acc[s, :, core * T:(core + 1) * T] * scale).astype(BF16)
    dq_copies = [
        remote(
            dq_send.at[rem(i + o, width)], dq_recv.at[i], dq_send_sem.at[o - 1], dq_recv_sem.at[i],
            me.at(i=rem(i + o, width)),
        )
        for o in range(1, width)
    ]
    for copy in dq_copies:
        copy.start()

    if me.halves > 1:
        away = 1 - me.half
        remote(iz.at[away], iz.at[away], iz_send_sem.at[0], iz_recv_sem.at[away], me.at(half=away)).wait_recv()
    summed = iz[0].astype(F32)
    for half in range(1, me.halves):
        summed = summed + iz[half].astype(F32)
    input_out[...] = summed * math.sqrt(SK / (x_ref.shape[1] * me.ys * me.halves))

    heads = me.ys * me.halves
    kv_factor = math.sqrt(SK / (F * heads))
    grad_out[SK:3 * SK, :] = dkv_send[0].astype(F32) * kv_factor

    def add_kv(b, carry):
        remote(dkv_send.at[0], dkv_recv.at[b], dkv_send_sem.at[0], dkv_recv_sem.at[b], me.at(z=rem(z + 1, planes))).wait_recv()
        grad_out[SK:3 * SK, :] += dkv_recv[b].astype(F32) * kv_factor
        return carry

    dq_recv[i] = dq_send[i]
    lax.fori_loop(z + 1, planes, add_kv, 0)
    for o in range(1, width):
        p = rem(i + o, width)
        remote(dq_send.at[p], dq_recv.at[p], dq_send_sem.at[0], dq_recv_sem.at[p], me.at(i=p)).wait_recv()
    query_sum = dq_recv[0].astype(F32)
    for p in range(1, width):
        query_sum = query_sum + dq_recv[p].astype(F32)
    grad_out[0:SK, :] = query_sum * math.sqrt(SK / (H * F * heads))
    grad_out[3 * SK:, :] = jnp.zeros((SK, T), F32)

    for copy in own_copies + ring_copies + list(sib_copies.values()) + iy_copies + st_copies + fin_copies + dq_copies:
        copy.wait_send()
    if me.halves > 1:
        iz_copy.wait_send()

    @pl.when(has_above)
    def _():
        def left_kv(b, carry):
            kv_copy(b).wait_send()
            return carry

        lax.fori_loop(0, z + 1, left_kv, 0)

    def left_dkv(k, carry):
        dkv_copy(k, z - k).wait_send()
        return carry

    lax.fori_loop(1, z + 1, left_dkv, 0)


def attention(layer_input, queries, key_states, value_states, out_grad, input_hash, query_hash, key_hash, value_hash):
    planes, chips, cores = SEQ_GRID
    ys, halves = HEAD_GRID
    width = chips * cores
    rows = 2 * T
    dma = pltpu.SemaphoreType.DMA
    vmem = pltpu.VMEM
    return pl.pallas_call(
        attention_kernel,
        out_shape=(jax.ShapeDtypeStruct((SK, T), F32), jax.ShapeDtypeStruct((4 * SK, T), F32)),
        in_specs=[pl.BlockSpec(memory_space=pltpu.VMEM)] * 9,
        out_specs=(pl.BlockSpec(memory_space=pltpu.VMEM),) * 2,
        scratch_shapes=[
            vmem((chips, 2, H, rows, F), BF16),
            vmem((planes, 2, T, F), BF16),
            vmem((chips, planes, T, H * rows), F32),
            vmem((chips, planes, T, H * rows), F32),
            vmem((chips, 8, H * rows), F32),
            vmem((planes, H * SK, T), BF16),
            vmem((width, 8, H * T), F32),
            vmem((width, 8, H * T), F32),
            vmem((width, 8, H * T), F32),
            vmem((chips, 8, H * rows), F32),
            vmem((chips, SK, rows), F32),
            vmem((2, T, F), F32),
            vmem((planes, 2 * SK, T), BF16),
            vmem((planes, 2 * SK, T), BF16),
            vmem((width, SK, T), BF16),
            vmem((width, SK, T), BF16),
            vmem((ys, SK, T), BF16),
            vmem((halves, SK, T), BF16),
            dma((chips, 2, 2)), dma((3, 2)), dma((2,)), dma((3, 2)),
            dma((planes,)), dma((planes,)),
            dma((width,)), dma((width,)), dma((width,)), dma((width,)),
            dma((planes,)), dma((planes,)),
            dma((width,)), dma((width,)),
            dma((ys,)), dma((ys,)), dma((halves,)), dma((halves,)),
        ],
        compiler_params=pltpu.CompilerParams(
            collective_id=0, has_side_effects=True, vmem_limit_bytes=56 * 1024 * 1024
        ),
        name="attention_backward",
    )(layer_input, queries, key_states, value_states, out_grad, input_hash, query_hash, key_hash, value_hash)


def documents_kernel(
    starts, targets, input_ref, grad_ref, out_ref,
    products, near, plane_docs, far_send, far,
    near_send_sem, near_recv_sem, plane_send_sem, plane_recv_sem, far_send_sem, far_recv_sem,
):
    me = Place()
    planes, width, ys, halves = me.planes, me.width, me.ys, me.halves
    i, z = me.i, me.z
    doc_count = starts.shape[0]
    place_in_group = lax.rem(i, GROUP)
    group_first = i - place_in_group
    band = SK // ys
    line = planes * halves

    near_peers = []
    for o in range(1, GROUP * ys):
        p = rem(place_in_group + o // ys, GROUP)
        y = rem(me.y + o % ys, ys)
        near_peers.append((p, y))
    far_peers = []
    for o in range(1, line):
        fz = rem(z + o // halves, planes)
        half = rem(me.half + o % halves, halves)
        far_peers.append((fz, half))
    friends = [me.at(i=rem(i + o, width)) for o in range(1, width)]
    friends += [me.at(i=group_first + p, y=y) for n, (p, y) in enumerate(near_peers) if (n + 1) % ys]
    friends += [me.at(z=fz, half=half) for fz, half in far_peers]
    barrier = pltpu.get_barrier_semaphore()
    for device in friends:
        pl.semaphore_signal(barrier, inc=1, device_id=device, device_id_type=MESH)

    group_tokens = GROUP * T
    tokens = lax.broadcasted_iota(jnp.int32, (1, T), 1)
    here = tokens + me.seq * T
    here_group = (me.seq // GROUP) * group_tokens
    slot_group = (z * (width // GROUP) + tokens // (2 * GROUP)) * group_tokens
    doc_of = jnp.zeros((1, T), jnp.int32)
    slot_first = jnp.zeros((1, T), jnp.int32)
    slot_past = jnp.zeros((1, T), jnp.int32)
    for d in range(doc_count):
        begins = starts[d]
        doc_of = doc_of + jnp.where(jnp.logical_and(begins <= here, begins > here_group), 1, 0)
        slot_first = slot_first + jnp.where(begins < slot_group, 1, 0)
        slot_past = slot_past + jnp.where(begins < slot_group + group_tokens, 1, 0)
    slot_doc = slot_first + lax.rem(tokens, 2 * GROUP)
    slot_doc = jnp.where(slot_doc < slot_past, slot_doc, -1)
    slot_row = jnp.full((1, T), -1, jnp.int32)
    for d in range(doc_count):
        slot_row = jnp.where(slot_doc == d, targets[d], slot_row)

    input_sketch = input_ref[...]
    masked = jnp.concatenate([jnp.where(doc_of == e, input_sketch, 0.0) for e in range(DOCS_MOST)], axis=0)
    grads = grad_ref[...]
    masked_high = masked.astype(BF16)
    masked_low = (masked - masked_high.astype(F32)).astype(BF16)
    grads_high = grads.astype(BF16)
    grads_low = (grads - grads_high.astype(F32)).astype(BF16)
    product = dot_nt(masked_high, grads_high) + (dot_nt(masked_high, grads_low) + dot_nt(masked_low, grads_high))
    products[...] = product.reshape(DOCS_MOST, SK, 4 * SK).astype(BF16)

    pl.semaphore_wait(barrier, len(friends))

    def part(p, y):
        return products.at[pl.ds(p * 2, 2), pl.ds(pl.multiple_of(y * band, band), band), :]

    my_slot = place_in_group * ys + me.y
    near_copies = [
        remote(part(p, y), near.at[my_slot], near_send_sem.at[n], near_recv_sem.at[my_slot], me.at(i=group_first + p, y=y))
        for n, (p, y) in enumerate(near_peers)
    ]
    for copy in near_copies:
        copy.start()
    summed = part(place_in_group, me.y)[...].astype(F32)
    for p, y in near_peers:
        slot = p * ys + y
        remote(near.at[slot], near.at[slot], near_send_sem.at[0], near_recv_sem.at[slot], me.at(i=group_first + p, y=y)).wait_recv()
        summed = summed + near[slot].astype(F32)
    plane_docs[i] = summed.astype(BF16)

    plane_copies = [
        remote(plane_docs.at[i], plane_docs.at[i], plane_send_sem.at[o - 1], plane_recv_sem.at[i], me.at(i=rem(i + o, width)))
        for o in range(1, width)
    ]
    for copy in plane_copies:
        copy.start()
    for o in range(1, width):
        p = rem(i + o, width)
        remote(plane_docs.at[p], plane_docs.at[p], plane_send_sem.at[0], plane_recv_sem.at[p], me.at(i=p)).wait_recv()

    def gather_row(fz, carry):
        row = fz * width + i
        found = jnp.zeros((band, 4 * SK), F32)
        for j in range(width):
            for e in range(2):
                chosen = jnp.broadcast_to(slot_row[:, 2 * j + e:2 * j + e + 1], (band, 4 * SK)) == row
                found = found + jnp.where(chosen, plane_docs[j, e].astype(F32), 0.0)
        own = band // halves
        for half in range(halves):
            rows_half = found[half * own:(half + 1) * own, :]
            both = jnp.concatenate([rows_half[:, 0:2 * SK], rows_half[:, 2 * SK:]], axis=0)
            far_send[fz * halves + half] = both.astype(BF16)
        return carry

    lax.fori_loop(0, planes, gather_row, 0)
    my_line = z * halves + me.half
    far_copies = [
        remote(far_send.at[fz * halves + half], far.at[my_line], far_send_sem.at[n], far_recv_sem.at[my_line], me.at(z=fz, half=half))
        for n, (fz, half) in enumerate(far_peers)
    ]
    for copy in far_copies:
        copy.start()
    result = far_send[my_line].astype(F32)
    for fz, half in far_peers:
        slot = fz * halves + half
        remote(far.at[slot], far.at[slot], far_send_sem.at[0], far_recv_sem.at[slot], me.at(z=fz, half=half)).wait_recv()
        result = result + far[slot].astype(F32)
    own = band // halves
    out_ref[...] = jnp.concatenate([result[0:own], result[own:]], axis=1)

    for copy in near_copies + plane_copies + far_copies:
        copy.wait_send()


def documents(input_sketch, grad_sketch, doc_starts, doc_rows):
    planes, chips, cores = SEQ_GRID
    ys, halves = HEAD_GRID
    width = chips * cores
    line = planes * halves
    band = SK // ys
    dma = pltpu.SemaphoreType.DMA
    vmem = pltpu.VMEM
    return pl.pallas_call(
        documents_kernel,
        out_shape=jax.ShapeDtypeStruct((band // halves, 4 * SK), F32),
        in_specs=[pl.BlockSpec(memory_space=pltpu.SMEM)] * 2 + [pl.BlockSpec(memory_space=pltpu.VMEM)] * 2,
        out_specs=pl.BlockSpec(memory_space=pltpu.VMEM),
        scratch_shapes=[
            vmem((DOCS_MOST, SK, 4 * SK), BF16),
            vmem((GROUP * ys, 2, band, 4 * SK), BF16),
            vmem((width, 2, band, 4 * SK), BF16),
            vmem((line, 2 * band // halves, 2 * SK), BF16),
            vmem((line, 2 * band // halves, 2 * SK), BF16),
            dma((GROUP * ys,)), dma((GROUP * ys,)),
            dma((width,)), dma((width,)),
            dma((line,)), dma((line,)),
        ],
        compiler_params=pltpu.CompilerParams(collective_id=1, has_side_effects=True),
        name="documents",
    )(doc_starts, doc_rows, input_sketch, grad_sketch)


def on_device(
    layer_input, queries, key_states, value_states, out_grad,
    input_hash, query_hash, key_hash, value_hash, doc_starts, doc_rows,
):
    input_sketch, grad_sketch = attention(
        layer_input, queries, key_states, value_states, out_grad, input_hash, query_hash, key_hash, value_hash
    )
    result = documents(input_sketch, grad_sketch, doc_starts, doc_rows)
    bands = result.shape[0]
    return result[:, :3 * SK].reshape(bands, 3, SK).transpose(1, 0, 2).reshape(1, 3, bands * SK)


def solution(mesh):
    return jax.shard_map(
        on_device,
        mesh=mesh,
        in_specs=(
            P("seq", "head"), P("seq", "head"), P("seq", "head"), P("seq", "head"), P("seq", "head"),
            P(None, "head"), P(None, "head"), P(None, "head"), P(None, "head"),
            P(), P(),
        ),
        out_specs=P("seq", None, "head"),
        check_vma=False,
    )
```

```python
import functools
import math

import jax
import jax.numpy as jnp
from jax import lax
from jax.experimental import pallas as pl
from jax.experimental.pallas import tpu as pltpu
from jax.sharding import PartitionSpec as P

SEQ_GRID = (8, 4, 2)
HEAD_GRID = (4, 2)

T = 128
F = 128
H = 4
SK = 64
GROUP = 4
DOCS_MOST = 8
LOW = -1e30
MESH = pl.DeviceIdType.MESH
F32 = jnp.float32
BF16 = jnp.bfloat16


def dot_nt(a, b):
    return lax.dot_general(a, b, (((1,), (1,)), ((), ())), preferred_element_type=F32)


def dot_nn(a, b):
    return jnp.dot(a, b, preferred_element_type=F32)


def sign_table(hashes):
    buckets = lax.broadcasted_iota(jnp.int32, (SK, hashes.shape[1]), 0)
    signs = (1 - 2 * (hashes[1:2, :] & 1)).astype(F32)
    return jnp.where(buckets == hashes[0:1, :], signs, 0.0).astype(BF16)


def rem(value, count):
    return lax.rem(value + count, count)


class Place:
    def __init__(self):
        self.planes, self.chips, self.cores = SEQ_GRID
        self.ys, self.halves = HEAD_GRID
        self.width = self.chips * self.cores
        seq = lax.axis_index("seq")
        head = lax.axis_index("head")
        self.seq, self.head = seq, head
        self.i = lax.rem(seq, self.width)
        self.z = seq // self.width
        self.c = lax.rem(self.i, self.cores)
        self.x = self.i // self.cores
        self.y = head // self.halves
        self.half = lax.rem(head, self.halves)

    def at(self, z=None, i=None, y=None, half=None):
        z = self.z if z is None else z
        i = self.i if i is None else i
        y = self.y if y is None else y
        half = self.half if half is None else half
        return (z * self.width + i, y * self.halves + half)


def remote(src, dst, send_sem, recv_sem, device):
    return pltpu.make_async_remote_copy(
        src_ref=src, dst_ref=dst, send_sem=send_sem, recv_sem=recv_sem, device_id=device, device_id_type=MESH
    )


def greet(devices):
    barrier = pltpu.get_barrier_semaphore()
    for device in devices:
        pl.semaphore_signal(barrier, inc=1, device_id=device, device_id_type=MESH)


def kernel(
    starts, targets, x_ref, q_ref, k_ref, v_ref, do_ref, xh_ref, qh_ref, kh_ref, vh_ref,
    out_ref,
    qall, kv, scores, wgrads, stat, kmt, stat_send, stat_recv, total, dq_acc, dkv_acc,
    dkv_send, dkv_recv, dq_send, dq_recv, iy, iz, grad_sum,
    products, near, plane_docs, far_send, far,
    q_recv, q_own, q_ring, q_sib, kv_send_sem, kv_recv_sem, st_send_sem, st_recv_sem,
    dkv_send_sem, dkv_recv_sem, dq_send_sem, dq_recv_sem, iy_send_sem, iy_recv_sem, iz_send_sem, iz_recv_sem,
    near_send_sem, near_recv_sem, plane_send_sem, plane_recv_sem, far_send_sem, far_recv_sem,
):
    me = Place()
    planes, chips, width = me.planes, me.chips, me.width
    x, c, z, i = me.x, me.c, me.z, me.i
    rows = 2 * T
    scale = 1.0 / math.sqrt(F)
    scale2 = scale * math.log2(math.e)

    ys, halves = me.ys, me.halves
    place_in_group = lax.rem(i, GROUP)
    group_first = i - place_in_group
    near_peers = []
    for o in range(1, GROUP * ys):
        near_peers.append((rem(place_in_group + o // ys, GROUP), rem(me.y + o % ys, ys)))
    far_peers = []
    for o in range(1, planes * halves):
        far_peers.append((rem(z + o // halves, planes), rem(me.half + o % halves, halves)))
    friends = [me.at(z=fz, half=half) for fz, half in far_peers]
    friends += [me.at(i=group_first + p, y=y) for n, (p, y) in enumerate(near_peers) if (n + 1) % ys]
    friends += [me.at(i=rem(i + o, width)) for o in range(1, width)]
    greet(friends)

    mine = pl.ds(pl.multiple_of(c * T, T), T)
    other = pl.ds(pl.multiple_of((1 - c) * T, T), T)
    for h in range(H):
        qall[x, 0, h, mine, :] = q_ref[:, h * F:(h + 1) * F]
        qall[x, 1, h, mine, :] = do_ref[:, h * F:(h + 1) * F]
    kv[z, 0] = k_ref[...]
    kv[z, 1] = v_ref[...]

    def piece(step, core, part):
        s = rem(x + step, chips)
        ref = qall.at[s, part, :, pl.ds(pl.multiple_of(core * T, T), T), :]
        return ref, q_recv.at[s, core, part]

    def send_piece(step, core, part, send_sem, target):
        ref, recv_sem = piece(step, core, part)
        return remote(ref, ref, send_sem, recv_sem, target)

    sibling = me.at(i=x * 2 + 1 - c)
    right = me.at(i=rem(x + 1, chips) * 2 + c)
    left = me.at(i=rem(x + chips - 1, chips) * 2 + c)
    own_copies = [
        send_piece(0, c, part, q_own.at[n, part], target)
        for n, target in enumerate((sibling, right, left)) for part in range(2)
    ]
    ring_copies = [
        send_piece(chips - 1, c, 0, q_ring.at[0], right),
        send_piece(1, c, 1, q_ring.at[1], left),
    ]
    sib_copies = {
        (step, part): send_piece(step, c, part, q_sib.at[step - 1, part], sibling)
        for step in (1, 2, 3) for part in range(2)
    }

    def wait_piece(step, core, part):
        ref, recv_sem = piece(step, core, part)
        remote(ref, ref, q_own.at[0, 0], recv_sem, sibling).wait_recv()

    def kv_copy(b, hops):
        return remote(
            kv.at[b], kv.at[b], kv_send_sem.at[b, hops - 1], kv_recv_sem.at[b], me.at(z=rem(z + hops, planes))
        )

    def relay_kv(b):
        @pl.when(z + 2 < planes)
        def _():
            kv_copy(b, 2).start()

        @pl.when(z + 1 < planes)
        def _():
            kv_copy(b, 1).start()

    input_part = dot_nt(sign_table(xh_ref[...]), x_ref[...])
    iy[me.y] = input_part.astype(BF16)
    query_table = sign_table(qh_ref[...])
    query_tables = jnp.concatenate([query_table[:, h * F:(h + 1) * F] for h in range(H)], axis=0)
    key_table = sign_table(kh_ref[...])
    value_table = sign_table(vh_ref[...])
    kmt[0] = dot_nt(query_tables, kv[z, 0]).astype(BF16)
    for s in range(chips):
        stat[s, 0:1, :] = jnp.full((1, H * rows), LOW, F32)
        stat[s, 1:3, :] = jnp.zeros((2, H * rows), F32)
    dq_acc[...] = jnp.zeros_like(dq_acc)
    dkv_acc[...] = jnp.zeros_like(dkv_acc)
    grad_sum[3 * SK:, :] = jnp.zeros((SK, T), F32)

    doc_count = starts.shape[0]
    group_tokens = GROUP * T
    tokens = lax.broadcasted_iota(jnp.int32, (1, T), 1)
    here = tokens + me.seq * T
    here_group = (me.seq // GROUP) * group_tokens
    slot_group = (z * (width // GROUP) + tokens // (2 * GROUP)) * group_tokens
    doc_of = jnp.zeros((1, T), jnp.int32)
    slot_first = jnp.zeros((1, T), jnp.int32)
    slot_past = jnp.zeros((1, T), jnp.int32)
    for d in range(doc_count):
        begins = starts[d]
        doc_of = doc_of + jnp.where(jnp.logical_and(begins <= here, begins > here_group), 1, 0)
        slot_first = slot_first + jnp.where(begins < slot_group, 1, 0)
        slot_past = slot_past + jnp.where(begins < slot_group + group_tokens, 1, 0)
    slot_doc = slot_first + lax.rem(tokens, 2 * GROUP)
    slot_doc = jnp.where(slot_doc < slot_past, slot_doc, -1)
    slot_row = jnp.full((1, T), -1, jnp.int32)
    for d in range(doc_count):
        slot_row = jnp.where(slot_doc == d, targets[d], slot_row)

    pl.semaphore_wait(pltpu.get_barrier_semaphore(), len(friends))

    relay_kv(z)
    for copy in own_copies:
        copy.start()

    iy_copies = [
        remote(iy.at[me.y], iy.at[me.y], iy_send_sem.at[o - 1], iy_recv_sem.at[me.y], me.at(y=rem(me.y + o, me.ys)))
        for o in range(1, me.ys)
    ]
    for copy in iy_copies:
        copy.start()
    iz_copy = remote(iz.at[me.half], iz.at[me.half], iz_send_sem.at[0], iz_recv_sem.at[me.half], me.at(half=1 - me.half))

    def input_over_y():
        for o in range(1, me.ys):
            y = rem(me.y + o, me.ys)
            remote(iy.at[y], iy.at[y], iy_send_sem.at[0], iy_recv_sem.at[y], me.at(y=y)).wait_recv()
        summed = iy[0].astype(F32)
        for y in range(1, me.ys):
            summed = summed + iy[y].astype(F32)
        iz[me.half] = summed.astype(BF16)
        if me.halves > 1:
            iz_copy.start()

    def first_unit(s, k, masked):
        b = z - k
        for h in range(H):
            cols = pl.ds(h * rows, rows)
            st = dot_nt(kv[b, 0], qall[s, 0, h]) * scale2
            if masked:
                key_place = lax.broadcasted_iota(jnp.int32, (T, rows), 0) + i * T
                query_place = lax.broadcasted_iota(jnp.int32, (T, rows), 1) + s * rows
                st = jnp.where(key_place <= query_place, st, LOW)
            dp = dot_nt(kv[b, 1], qall[s, 1, h])
            scores[s, k, :, cols] = st
            wgrads[s, k, :, cols] = dp
            old_top = stat[s, 0:1, cols]
            top = jnp.maximum(old_top, jnp.max(st, axis=0, keepdims=True))
            e = jnp.exp2(st - top)
            keep = jnp.exp2(old_top - top)
            stat[s, 0:1, cols] = top
            stat[s, 1:2, cols] = stat[s, 1:2, cols] * keep + jnp.sum(e, axis=0, keepdims=True)
            stat[s, 2:3, cols] = stat[s, 2:3, cols] * keep + jnp.sum(e * dp, axis=0, keepdims=True)

    def arrived_kv(t):
        b = z - t
        kv_copy(b, 1).wait_recv()
        kmt[t] = dot_nt(query_tables, kv[b, 0]).astype(BF16)

    def first_blocks(s, low, high):
        @pl.when(jnp.logical_and(low == 0, high > 0))
        def _():
            first_unit(s, 0, True)

        def over_blocks(k, carry):
            first_unit(s, k, False)
            return carry

        lax.fori_loop(jnp.maximum(low, 1), high, over_blocks, 0)

    def odd_arrivals(t):
        @pl.when(t <= z)
        def _():
            arrived_kv(t)

        @pl.when(t + 1 <= z)
        def _():
            arrived_kv(t + 1)
            relay_kv(z - t - 1)

    def first_step(t, carry):
        @pl.when(lax.rem(t, 2) == 1)
        def _():
            odd_arrivals(t)

        @pl.when(t == 0)
        def _():
            for part in range(2):
                wait_piece(0, 1 - c, part)

        @pl.when(t == 2)
        def _():
            for step in (chips - 1, 1):
                for part in range(2):
                    wait_piece(step, c, part)
                ring_copies[0 if step == chips - 1 else 1].start()
                for part in range(2):
                    sib_copies[(step, part)].start()

        @pl.when(t == 3)
        def _():
            for step in (chips - 1, 1):
                for part in range(2):
                    wait_piece(step, 1 - c, part)

        @pl.when(t == 4)
        def _():
            input_over_y()
            for part in range(2):
                wait_piece(2, c, part)
                sib_copies[(2, part)].start()

        def over_chips(r, carry):
            active = 3 * ((r + 1) // 2)
            low = jnp.where(t == active, 0, t)
            high = jnp.where(t >= active, jnp.minimum(t, z) + 1, 0)
            first_blocks(rem(x + r * (r + 1) // 2, chips), low, high)
            return carry

        return lax.fori_loop(0, chips - 1, over_chips, carry)

    lax.fori_loop(0, 6, first_step, 0)

    @pl.when(7 <= z)
    def _():
        arrived_kv(7)

    for part in range(2):
        wait_piece(2, 1 - c, part)

    pairs = chips // 2

    def stat_copies(g):
        return [
            remote(
                stat_send.at[g], stat_recv.at[g, i], st_send_sem.at[g, o - 1], st_recv_sem.at[g, i],
                me.at(i=rem(i + o, width)),
            )
            for o in range(1, width)
        ]

    def finish_chips(g, carry):
        def one_chip(n, carry):
            s = 2 * g + n
            first_blocks(s, jnp.where(s == rem(x + 2, chips), 0, 6), z + 1)
            return carry

        lax.fori_loop(0, 2, one_chip, 0)
        for n in range(2):
            stat_send[g, 3 * n:3 * n + 3, :] = stat[2 * g + n, 0:3, :]
        for copy in stat_copies(g):
            copy.start()
        stat_recv[g, i] = stat_send[g]
        return carry

    lax.fori_loop(0, pairs, finish_chips, 0)

    def add_statistics(g):
        for o in range(1, width):
            p = rem(i + o, width)
            remote(
                stat_send.at[g], stat_recv.at[g, p], st_send_sem.at[g, 0], st_recv_sem.at[g, p], me.at(i=p)
            ).wait_recv()
        for n in range(2):
            first = 3 * n
            top = stat_recv[g, 0, first:first + 1, :]
            for p in range(1, width):
                top = jnp.maximum(top, stat_recv[g, p, first:first + 1, :])
            weight_sum = jnp.zeros_like(top)
            delta_sum = jnp.zeros_like(top)
            for p in range(width):
                factor = jnp.exp2(stat_recv[g, p, first:first + 1, :] - top)
                weight_sum = weight_sum + stat_recv[g, p, first + 1:first + 2, :] * factor
                delta_sum = delta_sum + stat_recv[g, p, first + 2:first + 3, :] * factor
            total[2 * g + n, 0:1, :] = top + jnp.log2(weight_sum)
            total[2 * g + n, 1:2, :] = delta_sum / weight_sum

    def second_unit(s, k):
        lows, grads = [], []
        for h in range(H):
            cols = pl.ds(h * rows, rows)
            p = jnp.exp2(scores[s, k, :, cols] - total[s, 0:1, cols])
            g = p * (wgrads[s, k, :, cols] - total[s, 1:2, cols])
            lows.append(p.astype(BF16))
            g = g.astype(BF16)
            grads.append(g)
            dq_acc[s] += dot_nn(kmt[k, h * SK:(h + 1) * SK, :], g)
        low = jnp.concatenate(lows, axis=1)
        grad = jnp.concatenate(grads, axis=1)
        dkv_acc[k, 0] += dot_nn(grad, qall[s, 0].reshape(H * rows, F))
        dkv_acc[k, 1] += dot_nn(low, qall[s, 1].reshape(H * rows, F))

    def dkv_copy(k, b):
        return remote(dkv_send.at[k], dkv_recv.at[z], dkv_send_sem.at[k], dkv_recv_sem.at[z], me.at(z=b))

    def send_dq(g):
        for s in (2 * g, 2 * g + 1):
            for core in range(2):
                dq_send[s * 2 + core] = (dq_acc[s, :, core * T:(core + 1) * T] * scale).astype(BF16)
        for n in range(GROUP):
            p = GROUP * g + n

            @pl.when(p != i)
            def _():
                dq_copy(p).start()

    def dq_copy(p):
        return remote(dq_send.at[p], dq_recv.at[i], dq_send_sem.at[p], dq_recv_sem.at[i], me.at(i=p))

    for g in range(pairs - 1):
        add_statistics(g)

        def half_blocks(k, carry):
            def over_chips(n, carry):
                second_unit(2 * g + n, k)
                return carry

            return lax.fori_loop(0, 2, over_chips, carry)

        lax.fori_loop(0, z + 1, half_blocks, 0)
        send_dq(g)
    add_statistics(pairs - 1)

    def second_step(n, carry):
        k = z - n

        def over_chips(m, carry):
            second_unit(chips - 2 + m, k)
            return carry

        lax.fori_loop(0, 2, over_chips, 0)
        dkv_send[k, 0:SK, :] = dot_nt(key_table, (dkv_acc[k, 0] * scale).astype(BF16)).astype(BF16)
        dkv_send[k, SK:, :] = dot_nt(value_table, dkv_acc[k, 1].astype(BF16)).astype(BF16)

        @pl.when(k > 0)
        def _():
            dkv_copy(k, n).start()

        return carry

    lax.fori_loop(0, z + 1, second_step, 0)
    send_dq(pairs - 1)

    if me.halves > 1:
        away = 1 - me.half
        remote(iz.at[away], iz.at[away], iz_send_sem.at[0], iz_recv_sem.at[away], me.at(half=away)).wait_recv()
    summed = iz[0].astype(F32)
    for half in range(1, me.halves):
        summed = summed + iz[half].astype(F32)
    input_sketch = summed * math.sqrt(SK / (x_ref.shape[1] * ys * halves))

    heads = me.ys * me.halves
    kv_factor = math.sqrt(SK / (F * heads))
    grad_sum[SK:3 * SK, :] = dkv_send[0].astype(F32) * kv_factor

    def add_kv(b, carry):
        remote(dkv_send.at[0], dkv_recv.at[b], dkv_send_sem.at[0], dkv_recv_sem.at[b], me.at(z=rem(z + 1, planes))).wait_recv()
        grad_sum[SK:3 * SK, :] += dkv_recv[b].astype(F32) * kv_factor
        return carry

    dq_recv[i] = dq_send[i]
    lax.fori_loop(z + 1, planes, add_kv, 0)
    for o in range(1, width):
        p = rem(i + o, width)
        remote(dq_send.at[p], dq_recv.at[p], dq_send_sem.at[0], dq_recv_sem.at[p], me.at(i=p)).wait_recv()
    query_sum = dq_recv[0].astype(F32)
    for p in range(1, width):
        query_sum = query_sum + dq_recv[p].astype(F32)
    grad_sum[0:SK, :] = query_sum * math.sqrt(SK / (H * F * heads))

    band = SK // ys
    masked = jnp.concatenate([jnp.where(doc_of == e, input_sketch, 0.0) for e in range(DOCS_MOST)], axis=0)
    grads = grad_sum[...]
    masked_high = masked.astype(BF16)
    masked_low = (masked - masked_high.astype(F32)).astype(BF16)
    grads_high = grads.astype(BF16)
    grads_low = (grads - grads_high.astype(F32)).astype(BF16)
    product = dot_nt(masked_high, grads_high) + (dot_nt(masked_high, grads_low) + dot_nt(masked_low, grads_high))
    products[...] = product.reshape(DOCS_MOST, SK, 4 * SK).astype(BF16)

    def part(p, y):
        return products.at[pl.ds(p * 2, 2), pl.ds(pl.multiple_of(y * band, band), band), :]

    my_slot = place_in_group * ys + me.y
    near_copies = [
        remote(part(p, y), near.at[my_slot], near_send_sem.at[n], near_recv_sem.at[my_slot], me.at(i=group_first + p, y=y))
        for n, (p, y) in enumerate(near_peers)
    ]
    for copy in near_copies:
        copy.start()
    summed = part(place_in_group, me.y)[...].astype(F32)
    for p, y in near_peers:
        slot = p * ys + y
        remote(near.at[slot], near.at[slot], near_send_sem.at[0], near_recv_sem.at[slot], me.at(i=group_first + p, y=y)).wait_recv()
        summed = summed + near[slot].astype(F32)
    plane_docs[i] = summed.astype(BF16)

    plane_copies = [
        remote(plane_docs.at[i], plane_docs.at[i], plane_send_sem.at[o - 1], plane_recv_sem.at[i], me.at(i=rem(i + o, width)))
        for o in range(1, width)
    ]
    for copy in plane_copies:
        copy.start()
    for o in range(1, width):
        p = rem(i + o, width)
        remote(plane_docs.at[p], plane_docs.at[p], plane_send_sem.at[0], plane_recv_sem.at[p], me.at(i=p)).wait_recv()

    def gather_row(fz, carry):
        row = fz * width + i
        found = jnp.zeros((band, 4 * SK), F32)
        for j in range(width):
            for e in range(2):
                chosen = jnp.broadcast_to(slot_row[:, 2 * j + e:2 * j + e + 1], (band, 4 * SK)) == row
                found = found + jnp.where(chosen, plane_docs[j, e].astype(F32), 0.0)
        own = band // halves
        for half in range(halves):
            rows_half = found[half * own:(half + 1) * own, :]
            both = jnp.concatenate([rows_half[:, 0:2 * SK], rows_half[:, 2 * SK:]], axis=0)
            far_send[fz * halves + half] = both.astype(BF16)
        return carry

    lax.fori_loop(0, planes, gather_row, 0)
    my_line = z * halves + me.half
    far_copies = [
        remote(far_send.at[fz * halves + half], far.at[my_line], far_send_sem.at[n], far_recv_sem.at[my_line], me.at(z=fz, half=half))
        for n, (fz, half) in enumerate(far_peers)
    ]
    for copy in far_copies:
        copy.start()
    result = far_send[my_line].astype(F32)
    for fz, half in far_peers:
        slot = fz * halves + half
        remote(far.at[slot], far.at[slot], far_send_sem.at[0], far_recv_sem.at[slot], me.at(z=fz, half=half)).wait_recv()
        result = result + far[slot].astype(F32)
    own = band // halves
    out_ref[...] = jnp.concatenate([result[0:own], result[own:]], axis=1)

    for copy in own_copies + ring_copies + list(sib_copies.values()) + iy_copies + near_copies + plane_copies + far_copies:
        copy.wait_send()
    if me.halves > 1:
        iz_copy.wait_send()

    for g in range(pairs):
        for copy in stat_copies(g):
            copy.wait_send()
    for p in range(width):
        @pl.when(p != i)
        def _():
            dq_copy(p).wait_send()

    def left_kv(n, carry):
        b = z - 2 * n

        @pl.when(z + 2 < planes)
        def _():
            kv_copy(b, 2).wait_send()

        @pl.when(z + 1 < planes)
        def _():
            kv_copy(b, 1).wait_send()

        return carry

    lax.fori_loop(0, z // 2 + 1, left_kv, 0)

    def left_dkv(k, carry):
        dkv_copy(k, z - k).wait_send()
        return carry

    lax.fori_loop(1, z + 1, left_dkv, 0)


def sketches_of(
    doc_starts, doc_rows, layer_input, queries, key_states, value_states, out_grad,
    input_hash, query_hash, key_hash, value_hash,
):
    planes, chips, cores = SEQ_GRID
    ys, halves = HEAD_GRID
    width = chips * cores
    rows = 2 * T
    line = planes * halves
    band = SK // ys
    pairs = chips // 2
    dma = pltpu.SemaphoreType.DMA
    vmem = pltpu.VMEM
    return pl.pallas_call(
        kernel,
        out_shape=jax.ShapeDtypeStruct((band // halves, 4 * SK), F32),
        in_specs=[pl.BlockSpec(memory_space=pltpu.SMEM)] * 2 + [pl.BlockSpec(memory_space=pltpu.VMEM)] * 9,
        out_specs=pl.BlockSpec(memory_space=pltpu.VMEM),
        scratch_shapes=[
            vmem((chips, 2, H, rows, F), BF16),
            vmem((planes, 2, T, F), BF16),
            vmem((chips, planes, T, H * rows), F32),
            vmem((chips, planes, T, H * rows), F32),
            vmem((chips, 8, H * rows), F32),
            vmem((planes, H * SK, T), BF16),
            vmem((pairs, 8, H * rows), F32),
            vmem((pairs, width, 8, H * rows), F32),
            vmem((chips, 8, H * rows), F32),
            vmem((chips, SK, rows), F32),
            vmem((planes, 2, T, F), F32),
            vmem((planes, 2 * SK, T), BF16),
            vmem((planes, 2 * SK, T), BF16),
            vmem((width, SK, T), BF16),
            vmem((width, SK, T), BF16),
            vmem((ys, SK, T), BF16),
            vmem((halves, SK, T), BF16),
            vmem((4 * SK, T), F32),
            vmem((DOCS_MOST, SK, 4 * SK), BF16),
            vmem((GROUP * ys, 2, band, 4 * SK), BF16),
            vmem((width, 2, band, 4 * SK), BF16),
            vmem((line, 2 * band // halves, 2 * SK), BF16),
            vmem((line, 2 * band // halves, 2 * SK), BF16),
            dma((chips, 2, 2)), dma((3, 2)), dma((2,)), dma((3, 2)),
            dma((planes, 2)), dma((planes,)),
            dma((pairs, width)), dma((pairs, width)),
            dma((planes,)), dma((planes,)),
            dma((width,)), dma((width,)),
            dma((ys,)), dma((ys,)), dma((halves,)), dma((halves,)),
            dma((GROUP * ys,)), dma((GROUP * ys,)),
            dma((width,)), dma((width,)),
            dma((line,)), dma((line,)),
        ],
        compiler_params=pltpu.CompilerParams(
            collective_id=0, has_side_effects=True, vmem_limit_bytes=56 * 1024 * 1024
        ),
        name="sketches",
    )(
        doc_starts, doc_rows, layer_input, queries, key_states, value_states, out_grad,
        input_hash, query_hash, key_hash, value_hash,
    )


def on_device(
    layer_input, queries, key_states, value_states, out_grad,
    input_hash, query_hash, key_hash, value_hash, doc_starts, doc_rows,
):
    result = sketches_of(
        doc_starts, doc_rows, layer_input, queries, key_states, value_states, out_grad,
        input_hash, query_hash, key_hash, value_hash,
    )
    bands = result.shape[0]
    return result[:, :3 * SK].reshape(bands, 3, SK).transpose(1, 0, 2).reshape(1, 3, bands * SK)


def solution(mesh):
    return jax.shard_map(
        on_device,
        mesh=mesh,
        in_specs=(
            P("seq", "head"), P("seq", "head"), P("seq", "head"), P("seq", "head"), P("seq", "head"),
            P(None, "head"), P(None, "head"), P(None, "head"), P(None, "head"),
            P(), P(),
        ),
        out_specs=P("seq", None, "head"),
        check_vma=False,
    )
```

```python
import functools
import math

import jax
import jax.numpy as jnp
from jax import lax
from jax.experimental import pallas as pl
from jax.experimental.pallas import tpu as pltpu
from jax.sharding import PartitionSpec as P

SEQ_GRID = (8, 4, 2)
HEAD_GRID = (4, 2)

T = 128
F = 128
H = 4
SK = 64
GROUP = 4
DOCS_MOST = 8
LOW = -1e30
MESH = pl.DeviceIdType.MESH
F32 = jnp.float32
BF16 = jnp.bfloat16


def dot_nt(a, b):
    return lax.dot_general(a, b, (((1,), (1,)), ((), ())), preferred_element_type=F32)


def dot_nn(a, b):
    return jnp.dot(a, b, preferred_element_type=F32)


def sign_table(hashes):
    buckets = lax.broadcasted_iota(jnp.int32, (SK, hashes.shape[1]), 0)
    signs = (1 - 2 * (hashes[1:2, :] & 1)).astype(F32)
    return jnp.where(buckets == hashes[0:1, :], signs, 0.0).astype(BF16)


def rem(value, count):
    return lax.rem(value + count, count)


class Place:
    def __init__(self):
        self.planes, self.chips, self.cores = SEQ_GRID
        self.ys, self.halves = HEAD_GRID
        self.width = self.chips * self.cores
        seq = lax.axis_index("seq")
        head = lax.axis_index("head")
        self.seq, self.head = seq, head
        self.i = lax.rem(seq, self.width)
        self.z = seq // self.width
        self.c = lax.rem(self.i, self.cores)
        self.x = self.i // self.cores
        self.y = head // self.halves
        self.half = lax.rem(head, self.halves)

    def at(self, z=None, i=None, y=None, half=None):
        z = self.z if z is None else z
        i = self.i if i is None else i
        y = self.y if y is None else y
        half = self.half if half is None else half
        return (z * self.width + i, y * self.halves + half)


def remote(src, dst, send_sem, recv_sem, device):
    return pltpu.make_async_remote_copy(
        src_ref=src, dst_ref=dst, send_sem=send_sem, recv_sem=recv_sem, device_id=device, device_id_type=MESH
    )


def greet(devices):
    barrier = pltpu.get_barrier_semaphore()
    for device in devices:
        pl.semaphore_signal(barrier, inc=1, device_id=device, device_id_type=MESH)


def kernel(
    starts, targets, x_ref, q_ref, k_ref, v_ref, do_ref, xh_ref, qh_ref, kh_ref, vh_ref,
    out_ref,
    qall, kv, scores, wgrads, stat, kmt, stat_send, stat_recv, total, dq_acc, dkv_acc,
    dkv_send, dkv_recv, dq_send, dq_recv, iy, iz, grad_sum,
    products, near, plane_docs, far_send, far,
    inputs, input_sem, hello, q_recv, q_own, q_ring, q_sib, kv_send_sem, kv_recv_sem, st_send_sem, st_recv_sem,
    dkv_send_sem, dkv_recv_sem, dq_send_sem, dq_recv_sem, iy_send_sem, iy_recv_sem, iz_send_sem, iz_recv_sem,
    near_send_sem, near_recv_sem, plane_send_sem, plane_recv_sem, far_send_sem, far_recv_sem,
):
    me = Place()
    planes, chips, width = me.planes, me.chips, me.width
    x, c, z, i = me.x, me.c, me.z, me.i
    rows = 2 * T
    scale = 1.0 / math.sqrt(F)
    scale2 = scale * math.log2(math.e)

    ys, halves = me.ys, me.halves
    place_in_group = lax.rem(i, GROUP)
    group_first = i - place_in_group
    near_peers = []
    for o in range(1, GROUP * ys):
        near_peers.append((rem(place_in_group + o // ys, GROUP), rem(me.y + o % ys, ys)))
    far_peers = []
    for o in range(1, planes * halves):
        far_peers.append((rem(z + o // halves, planes), rem(me.half + o % halves, halves)))
    line = planes * halves

    def along(steps):
        to = rem(me.half * planes + z + steps, line)
        return me.at(z=lax.rem(to, planes), half=to // planes)

    friends = [along(o) for o in sorted({o % line for o in (1, 2, -1, -2)} - {0})]
    hellos = 3 if line > 5 else 0

    def pass_hello(n):
        for steps in (2, -2):
            pl.semaphore_signal(hello.at[n], inc=1, device_id=along(steps), device_id_type=MESH)

    def hear_hello(n):
        pl.semaphore_wait(hello.at[n], 2)

    friends += [me.at(i=group_first + p, y=y) for n, (p, y) in enumerate(near_peers) if (n + 1) % ys]
    friends += [me.at(i=rem(i + o, width)) for o in range(1, width)]
    greet(friends)

    mine = pl.ds(pl.multiple_of(c * T, T), T)
    loads = [pltpu.make_async_copy(k_ref, kv.at[z, 0], input_sem.at[0]), pltpu.make_async_copy(v_ref, kv.at[z, 1], input_sem.at[1])]
    for part, ref in enumerate((q_ref, do_ref)):
        for h in range(H):
            loads.append(
                pltpu.make_async_copy(
                    ref.at[:, pl.ds(h * F, F)], qall.at[x, part, h, mine, :], input_sem.at[2 + part * H + h]
                )
            )
    load_input = pltpu.make_async_copy(x_ref, inputs, input_sem.at[2 + 2 * H])
    for load in loads:
        load.start()
    load_input.start()
    for load in loads:
        load.wait()

    def piece(step, core, part):
        s = rem(x + step, chips)
        ref = qall.at[s, part, :, pl.ds(pl.multiple_of(core * T, T), T), :]
        return ref, q_recv.at[s, core, part]

    def send_piece(step, core, part, send_sem, target):
        ref, recv_sem = piece(step, core, part)
        return remote(ref, ref, send_sem, recv_sem, target)

    sibling = me.at(i=x * 2 + 1 - c)
    right = me.at(i=rem(x + 1, chips) * 2 + c)
    left = me.at(i=rem(x + chips - 1, chips) * 2 + c)
    own_copies = [
        send_piece(0, c, part, q_own.at[n, part], target)
        for n, target in enumerate((sibling, right, left)) for part in range(2)
    ]
    ring_copies = [
        send_piece(chips - 1, c, 0, q_ring.at[0], right),
        send_piece(1, c, 1, q_ring.at[1], left),
    ]
    sib_copies = {
        (step, part): send_piece(step, c, part, q_sib.at[step - 1, part], sibling)
        for step in (1, 2, 3) for part in range(2)
    }

    def wait_piece(step, core, part):
        ref, recv_sem = piece(step, core, part)
        remote(ref, ref, q_own.at[0, 0], recv_sem, sibling).wait_recv()

    def kv_copy(b, hops, part):
        return remote(
            kv.at[b, part], kv.at[b, part], kv_send_sem.at[b, hops - 1, part], kv_recv_sem.at[b, part],
            me.at(z=rem(z + hops, planes)),
        )

    def relay_kv(b, part):
        @pl.when(z + 2 < planes)
        def _():
            kv_copy(b, 2, part).start()

        @pl.when(z + 1 < planes)
        def _():
            kv_copy(b, 1, part).start()

    pl.semaphore_wait(pltpu.get_barrier_semaphore(), len(friends))

    for part in range(2):
        relay_kv(z, part)
    for target, part in ((1, 0), (2, 1), (0, 0), (0, 1), (1, 1), (2, 0)):
        own_copies[2 * target + part].start()

    if hellos:
        pass_hello(0)
    load_input.wait()

    input_part = dot_nt(sign_table(xh_ref[...]), inputs[...])
    iy[me.y] = input_part.astype(BF16)
    query_table = sign_table(qh_ref[...])
    query_tables = jnp.concatenate([query_table[:, h * F:(h + 1) * F] for h in range(H)], axis=0)
    key_table = sign_table(kh_ref[...])
    value_table = sign_table(vh_ref[...])
    kmt[0] = dot_nt(query_tables, kv[z, 0]).astype(BF16)
    for s in range(chips):
        stat[s, 0:1, :] = jnp.full((1, H * rows), LOW, F32)
        stat[s, 1:3, :] = jnp.zeros((2, H * rows), F32)
    dq_acc[...] = jnp.zeros_like(dq_acc)
    dkv_acc[...] = jnp.zeros_like(dkv_acc)
    grad_sum[3 * SK:, :] = jnp.zeros((SK, T), F32)

    doc_count = starts.shape[0]
    group_tokens = GROUP * T
    tokens = lax.broadcasted_iota(jnp.int32, (1, T), 1)
    here = tokens + me.seq * T
    here_group = (me.seq // GROUP) * group_tokens
    slot_group = (z * (width // GROUP) + tokens // (2 * GROUP)) * group_tokens
    doc_of = jnp.zeros((1, T), jnp.int32)
    slot_first = jnp.zeros((1, T), jnp.int32)
    slot_past = jnp.zeros((1, T), jnp.int32)
    for d in range(doc_count):
        begins = starts[d]
        doc_of = doc_of + jnp.where(jnp.logical_and(begins <= here, begins > here_group), 1, 0)
        slot_first = slot_first + jnp.where(begins < slot_group, 1, 0)
        slot_past = slot_past + jnp.where(begins < slot_group + group_tokens, 1, 0)
    slot_doc = slot_first + lax.rem(tokens, 2 * GROUP)
    slot_doc = jnp.where(slot_doc < slot_past, slot_doc, -1)
    slot_row = jnp.full((1, T), -1, jnp.int32)
    for d in range(doc_count):
        slot_row = jnp.where(slot_doc == d, targets[d], slot_row)

    iy_copies = [
        remote(iy.at[me.y], iy.at[me.y], iy_send_sem.at[o - 1], iy_recv_sem.at[me.y], me.at(y=rem(me.y + o, me.ys)))
        for o in range(1, me.ys)
    ]
    for copy in iy_copies:
        copy.start()
    iz_copy = remote(iz.at[me.half], iz.at[me.half], iz_send_sem.at[0], iz_recv_sem.at[me.half], me.at(half=1 - me.half))

    def input_over_y():
        for o in range(1, me.ys):
            y = rem(me.y + o, me.ys)
            remote(iy.at[y], iy.at[y], iy_send_sem.at[0], iy_recv_sem.at[y], me.at(y=y)).wait_recv()
        summed = iy[0].astype(F32)
        for y in range(1, me.ys):
            summed = summed + iy[y].astype(F32)
        iz[me.half] = summed.astype(BF16)

    def first_unit(s, k, masked):
        b = z - k
        for h in range(H):
            cols = pl.ds(h * rows, rows)
            st = dot_nt(kv[b, 0], qall[s, 0, h]) * scale2
            if masked:
                key_place = lax.broadcasted_iota(jnp.int32, (T, rows), 0) + i * T
                query_place = lax.broadcasted_iota(jnp.int32, (T, rows), 1) + s * rows
                st = jnp.where(key_place <= query_place, st, LOW)
            dp = dot_nt(kv[b, 1], qall[s, 1, h])
            scores[s, k, :, cols] = st
            wgrads[s, k, :, cols] = dp
            old_top = stat[s, 0:1, cols]
            top = jnp.maximum(old_top, jnp.max(st, axis=0, keepdims=True))
            e = jnp.exp2(st - top)
            keep = jnp.exp2(old_top - top)
            stat[s, 0:1, cols] = top
            stat[s, 1:2, cols] = stat[s, 1:2, cols] * keep + jnp.sum(e, axis=0, keepdims=True)
            stat[s, 2:3, cols] = stat[s, 2:3, cols] * keep + jnp.sum(e * dp, axis=0, keepdims=True)

    def arrived_kv(t):
        for part in range(2):
            kv_copy(z - t, 1, part).wait_recv()

    def sketch_keys(t):
        kmt[t] = dot_nt(query_tables, kv[z - t, 0]).astype(BF16)

    def first_blocks(s, low, high):
        @pl.when(jnp.logical_and(low == 0, high > 0))
        def _():
            first_unit(s, 0, True)

        def over_blocks(k, carry):
            first_unit(s, k, False)
            return carry

        lax.fori_loop(jnp.maximum(low, 1), high, over_blocks, 0)

    def odd_arrivals(t):
        @pl.when(t + 1 <= z)
        def _():
            for part in range(2):
                kv_copy(z - t - 1, 1, part).wait_recv()
                relay_kv(z - t - 1, part)

        @pl.when(t <= z)
        def _():
            arrived_kv(t)
            sketch_keys(t)

        @pl.when(t + 1 <= z)
        def _():
            sketch_keys(t + 1)

    def first_step(t, carry):
        @pl.when(lax.rem(t, 2) == 1)
        def _():
            odd_arrivals(t)

        @pl.when(t == 0)
        def _():
            for part in range(2):
                wait_piece(0, 1 - c, part)

        if hellos:
            for n in (1, 2):
                @pl.when(t == 2 * n)
                def _():
                    hear_hello(n - 1)
                    pass_hello(n)

        @pl.when(t == 2)
        def _():
            for n, (step, part) in enumerate(((chips - 1, 0), (1, 1), (chips - 1, 1), (1, 0))):
                wait_piece(step, c, part)
                if n < 2:
                    ring_copies[n].start()
                sib_copies[(step, part)].start()

        @pl.when(t == 3)
        def _():
            for step in (chips - 1, 1):
                for part in range(2):
                    wait_piece(step, 1 - c, part)

        @pl.when(t == 4)
        def _():
            input_over_y()
            for part in range(2):
                wait_piece(2, c, part)
                sib_copies[(2, part)].start()

        def over_chips(r, carry):
            active = 3 * ((r + 1) // 2)
            low = jnp.where(t == active, 0, t)
            high = jnp.where(t >= active, jnp.minimum(t, z) + 1, 0)
            first_blocks(rem(x + r * (r + 1) // 2, chips), low, high)
            return carry

        return lax.fori_loop(0, chips - 1, over_chips, carry)

    lax.fori_loop(0, 6, first_step, 0)

    @pl.when(7 <= z)
    def _():
        arrived_kv(7)
        sketch_keys(7)

    for part in range(2):
        wait_piece(2, 1 - c, part)

    pairs = chips // 2

    def stat_copies(g):
        return [
            remote(
                stat_send.at[g], stat_recv.at[g, i], st_send_sem.at[g, o - 1], st_recv_sem.at[g, i],
                me.at(i=rem(i + o, width)),
            )
            for o in range(1, width)
        ]

    def finish_chips(g, carry):
        def one_chip(n, carry):
            s = 2 * g + n
            first_blocks(s, jnp.where(s == rem(x + 2, chips), 0, 6), z + 1)
            return carry

        lax.fori_loop(0, 2, one_chip, 0)
        for n in range(2):
            stat_send[g, 3 * n:3 * n + 3, :] = stat[2 * g + n, 0:3, :]
        for copy in stat_copies(g):
            copy.start()
        stat_recv[g, i] = stat_send[g]
        return carry

    lax.fori_loop(0, pairs, finish_chips, 0)
    if hellos:
        hear_hello(2)
    if me.halves > 1:
        iz_copy.start()

    def add_statistics(g):
        for o in range(1, width):
            p = rem(i + o, width)
            remote(
                stat_send.at[g], stat_recv.at[g, p], st_send_sem.at[g, 0], st_recv_sem.at[g, p], me.at(i=p)
            ).wait_recv()
        for n in range(2):
            first = 3 * n
            top = stat_recv[g, 0, first:first + 1, :]
            for p in range(1, width):
                top = jnp.maximum(top, stat_recv[g, p, first:first + 1, :])
            weight_sum = jnp.zeros_like(top)
            delta_sum = jnp.zeros_like(top)
            for p in range(width):
                factor = jnp.exp2(stat_recv[g, p, first:first + 1, :] - top)
                weight_sum = weight_sum + stat_recv[g, p, first + 1:first + 2, :] * factor
                delta_sum = delta_sum + stat_recv[g, p, first + 2:first + 3, :] * factor
            total[2 * g + n, 0:1, :] = top + jnp.log2(weight_sum)
            total[2 * g + n, 1:2, :] = delta_sum / weight_sum

    def second_unit(s, k):
        lows, grads = [], []
        for h in range(H):
            cols = pl.ds(h * rows, rows)
            p = jnp.exp2(scores[s, k, :, cols] - total[s, 0:1, cols])
            g = p * (wgrads[s, k, :, cols] - total[s, 1:2, cols])
            lows.append(p.astype(BF16))
            g = g.astype(BF16)
            grads.append(g)
            dq_acc[s] += dot_nn(kmt[k, h * SK:(h + 1) * SK, :], g)
        low = jnp.concatenate(lows, axis=1)
        grad = jnp.concatenate(grads, axis=1)
        dkv_acc[k, 0] += dot_nn(grad, qall[s, 0].reshape(H * rows, F))
        dkv_acc[k, 1] += dot_nn(low, qall[s, 1].reshape(H * rows, F))

    def dkv_copy(k, b):
        return remote(dkv_send.at[k], dkv_recv.at[z], dkv_send_sem.at[k], dkv_recv_sem.at[z], me.at(z=b))

    def send_dq(g):
        for s in (2 * g, 2 * g + 1):
            for core in range(2):
                dq_send[s * 2 + core] = (dq_acc[s, :, core * T:(core + 1) * T] * scale).astype(BF16)
        for n in range(GROUP):
            p = GROUP * g + n

            @pl.when(p != i)
            def _():
                dq_copy(p).start()

    def dq_copy(p):
        return remote(dq_send.at[p], dq_recv.at[i], dq_send_sem.at[p], dq_recv_sem.at[i], me.at(i=p))

    near_blocks = (z + 2) // 2
    add_statistics(0)

    def half_blocks(k, carry):
        def over_chips(s, carry):
            second_unit(s, k)
            return carry

        return lax.fori_loop(0, 2, over_chips, carry)

    lax.fori_loop(0, near_blocks, half_blocks, 0)
    add_statistics(1)

    def second_step(n, carry):
        k = z - n

        @pl.when(k == near_blocks - 1)
        def _():
            send_dq(0)

        def over_chips(s, carry):
            second_unit(s, k)
            return carry

        lax.fori_loop(jnp.where(k < near_blocks, 2, 0), chips, over_chips, 0)
        dkv_send[k, 0:SK, :] = dot_nt(key_table, (dkv_acc[k, 0] * scale).astype(BF16)).astype(BF16)
        dkv_send[k, SK:, :] = dot_nt(value_table, dkv_acc[k, 1].astype(BF16)).astype(BF16)

        @pl.when(k > 0)
        def _():
            dkv_copy(k, n).start()

        return carry

    lax.fori_loop(0, z + 1, second_step, 0)
    send_dq(1)

    if me.halves > 1:
        away = 1 - me.half
        remote(iz.at[away], iz.at[away], iz_send_sem.at[0], iz_recv_sem.at[away], me.at(half=away)).wait_recv()
    summed = iz[0].astype(F32)
    for half in range(1, me.halves):
        summed = summed + iz[half].astype(F32)
    input_sketch = summed * math.sqrt(SK / (x_ref.shape[1] * ys * halves))

    heads = me.ys * me.halves
    kv_factor = math.sqrt(SK / (F * heads))
    grad_sum[SK:3 * SK, :] = dkv_send[0].astype(F32) * kv_factor

    def add_kv(b, carry):
        remote(dkv_send.at[0], dkv_recv.at[b], dkv_send_sem.at[0], dkv_recv_sem.at[b], me.at(z=rem(z + 1, planes))).wait_recv()
        grad_sum[SK:3 * SK, :] += dkv_recv[b].astype(F32) * kv_factor
        return carry

    dq_recv[i] = dq_send[i]
    lax.fori_loop(z + 1, planes, add_kv, 0)
    for o in range(1, width):
        p = rem(i + o, width)
        remote(dq_send.at[p], dq_recv.at[p], dq_send_sem.at[0], dq_recv_sem.at[p], me.at(i=p)).wait_recv()
    query_sum = dq_recv[0].astype(F32)
    for p in range(1, width):
        query_sum = query_sum + dq_recv[p].astype(F32)
    grad_sum[0:SK, :] = query_sum * math.sqrt(SK / (H * F * heads))

    band = SK // ys
    masked = jnp.concatenate([jnp.where(doc_of == e, input_sketch, 0.0) for e in range(DOCS_MOST)], axis=0)
    grads = grad_sum[...]
    masked_high = masked.astype(BF16)
    masked_low = (masked - masked_high.astype(F32)).astype(BF16)
    grads_high = grads.astype(BF16)
    grads_low = (grads - grads_high.astype(F32)).astype(BF16)
    product = dot_nt(masked_high, grads_high) + (dot_nt(masked_high, grads_low) + dot_nt(masked_low, grads_high))
    products[...] = product.reshape(DOCS_MOST, SK, 4 * SK).astype(BF16)

    def part(p, y):
        return products.at[pl.ds(p * 2, 2), pl.ds(pl.multiple_of(y * band, band), band), :]

    my_slot = place_in_group * ys + me.y
    near_copies = [
        remote(part(p, y), near.at[my_slot], near_send_sem.at[n], near_recv_sem.at[my_slot], me.at(i=group_first + p, y=y))
        for n, (p, y) in enumerate(near_peers)
    ]
    for copy in near_copies:
        copy.start()
    summed = part(place_in_group, me.y)[...].astype(F32)
    for p, y in near_peers:
        slot = p * ys + y
        remote(near.at[slot], near.at[slot], near_send_sem.at[0], near_recv_sem.at[slot], me.at(i=group_first + p, y=y)).wait_recv()
        summed = summed + near[slot].astype(F32)
    plane_docs[i] = summed.astype(BF16)

    plane_copies = [
        remote(plane_docs.at[i], plane_docs.at[i], plane_send_sem.at[o - 1], plane_recv_sem.at[i], me.at(i=rem(i + o, width)))
        for o in range(1, width)
    ]
    for copy in plane_copies:
        copy.start()
    for o in range(1, width):
        p = rem(i + o, width)
        remote(plane_docs.at[p], plane_docs.at[p], plane_send_sem.at[0], plane_recv_sem.at[p], me.at(i=p)).wait_recv()

    def gather_row(fz, carry):
        row = fz * width + i
        found = jnp.zeros((band, 4 * SK), F32)
        for j in range(width):
            for e in range(2):
                chosen = jnp.broadcast_to(slot_row[:, 2 * j + e:2 * j + e + 1], (band, 4 * SK)) == row
                found = found + jnp.where(chosen, plane_docs[j, e].astype(F32), 0.0)
        own = band // halves
        for half in range(halves):
            rows_half = found[half * own:(half + 1) * own, :]
            both = jnp.concatenate([rows_half[:, 0:2 * SK], rows_half[:, 2 * SK:]], axis=0)
            far_send[fz * halves + half] = both.astype(BF16)
        return carry

    lax.fori_loop(0, planes, gather_row, 0)
    my_line = z * halves + me.half
    far_copies = [
        remote(far_send.at[fz * halves + half], far.at[my_line], far_send_sem.at[n], far_recv_sem.at[my_line], me.at(z=fz, half=half))
        for n, (fz, half) in enumerate(far_peers)
    ]
    for copy in far_copies:
        copy.start()
    result = far_send[my_line].astype(F32)
    for fz, half in far_peers:
        slot = fz * halves + half
        remote(far.at[slot], far.at[slot], far_send_sem.at[0], far_recv_sem.at[slot], me.at(z=fz, half=half)).wait_recv()
        result = result + far[slot].astype(F32)
    own = band // halves
    query_key, value_only = result[0:own], result[own:]
    key_query, moved_value = pltpu.roll(query_key, SK, 1), pltpu.roll(value_only, SK, 1)
    first_half = lax.broadcasted_iota(jnp.int32, (1, 2 * SK), 1) < SK
    for p, (even, odd) in enumerate(((query_key, key_query), (key_query, query_key), (value_only, moved_value))):
        for pair in range(own // 2):
            out_ref[0, p:p + 1, pair * 2 * SK:(pair + 1) * 2 * SK] = jnp.where(
                first_half, even[2 * pair:2 * pair + 1], odd[2 * pair + 1:2 * pair + 2]
            )

    for copy in own_copies + ring_copies + list(sib_copies.values()) + iy_copies + near_copies + plane_copies + far_copies:
        copy.wait_send()
    if me.halves > 1:
        iz_copy.wait_send()

    for g in range(pairs):
        for copy in stat_copies(g):
            copy.wait_send()
    for p in range(width):
        @pl.when(p != i)
        def _():
            dq_copy(p).wait_send()

    def left_kv(n, carry):
        b = z - 2 * n

        for part in range(2):
            @pl.when(z + 2 < planes)
            def _():
                kv_copy(b, 2, part).wait_send()

            @pl.when(z + 1 < planes)
            def _():
                kv_copy(b, 1, part).wait_send()

        return carry

    lax.fori_loop(0, z // 2 + 1, left_kv, 0)

    def left_dkv(k, carry):
        dkv_copy(k, z - k).wait_send()
        return carry

    lax.fori_loop(1, z + 1, left_dkv, 0)


def sketches_of(
    doc_starts, doc_rows, layer_input, queries, key_states, value_states, out_grad,
    input_hash, query_hash, key_hash, value_hash,
):
    planes, chips, cores = SEQ_GRID
    ys, halves = HEAD_GRID
    width = chips * cores
    rows = 2 * T
    line = planes * halves
    band = SK // ys
    pairs = chips // 2
    dma = pltpu.SemaphoreType.DMA
    vmem = pltpu.VMEM
    return pl.pallas_call(
        kernel,
        out_shape=jax.ShapeDtypeStruct((1, 3, band // halves * SK), F32),
        in_specs=[pl.BlockSpec(memory_space=pltpu.SMEM)] * 2 + [pl.BlockSpec(memory_space=pl.ANY)] * 5
        + [pl.BlockSpec(memory_space=pltpu.VMEM)] * 4,
        out_specs=pl.BlockSpec(memory_space=pltpu.VMEM),
        scratch_shapes=[
            vmem((chips, 2, H, rows, F), BF16),
            vmem((planes, 2, T, F), BF16),
            vmem((chips, planes, T, H * rows), F32),
            vmem((chips, planes, T, H * rows), F32),
            vmem((chips, 8, H * rows), F32),
            vmem((planes, H * SK, T), BF16),
            vmem((pairs, 8, H * rows), F32),
            vmem((pairs, width, 8, H * rows), F32),
            vmem((chips, 8, H * rows), F32),
            vmem((chips, SK, rows), F32),
            vmem((planes, 2, T, F), F32),
            vmem((planes, 2 * SK, T), BF16),
            vmem((planes, 2 * SK, T), BF16),
            vmem((width, SK, T), BF16),
            vmem((width, SK, T), BF16),
            vmem((ys, SK, T), BF16),
            vmem((halves, SK, T), BF16),
            vmem((4 * SK, T), F32),
            vmem((DOCS_MOST, SK, 4 * SK), BF16),
            vmem((GROUP * ys, 2, band, 4 * SK), BF16),
            vmem((width, 2, band, 4 * SK), BF16),
            vmem((line, 2 * band // halves, 2 * SK), BF16),
            vmem((line, 2 * band // halves, 2 * SK), BF16),
            vmem(layer_input.shape, BF16),
            dma((2 + 2 * H + 1,)), pltpu.SemaphoreType.REGULAR((3,)),
            dma((chips, 2, 2)), dma((3, 2)), dma((2,)), dma((3, 2)),
            dma((planes, 2, 2)), dma((planes, 2)),
            dma((pairs, width)), dma((pairs, width)),
            dma((planes,)), dma((planes,)),
            dma((width,)), dma((width,)),
            dma((ys,)), dma((ys,)), dma((halves,)), dma((halves,)),
            dma((GROUP * ys,)), dma((GROUP * ys,)),
            dma((width,)), dma((width,)),
            dma((line,)), dma((line,)),
        ],
        compiler_params=pltpu.CompilerParams(
            collective_id=0, has_side_effects=True, vmem_limit_bytes=56 * 1024 * 1024
        ),
        name="sketches",
    )(
        doc_starts, doc_rows, layer_input, queries, key_states, value_states, out_grad,
        input_hash, query_hash, key_hash, value_hash,
    )


def on_device(
    layer_input, queries, key_states, value_states, out_grad,
    input_hash, query_hash, key_hash, value_hash, doc_starts, doc_rows,
):
    return sketches_of(
        doc_starts, doc_rows, layer_input, queries, key_states, value_states, out_grad,
        input_hash, query_hash, key_hash, value_hash,
    )


def solution(mesh):
    return jax.shard_map(
        on_device,
        mesh=mesh,
        in_specs=(
            P("seq", "head"), P("seq", "head"), P("seq", "head"), P("seq", "head"), P("seq", "head"),
            P(None, "head"), P(None, "head"), P(None, "head"), P(None, "head"),
            P(), P(),
        ),
        out_specs=P("seq", None, "head"),
        check_vma=False,
    )
```

```python
import functools
import math

import jax
import jax.numpy as jnp
from jax import lax
from jax.experimental import pallas as pl
from jax.experimental.pallas import tpu as pltpu
from jax.sharding import PartitionSpec as P

SEQ_GRID = (8, 4, 2)
HEAD_GRID = (4, 2)

T = 128
F = 128
H = 4
SK = 64
GROUP = 4
DOCS_MOST = 8
LOW = -1e30
MESH = pl.DeviceIdType.MESH
F32 = jnp.float32
BF16 = jnp.bfloat16


def dot_nt(a, b):
    return lax.dot_general(a, b, (((1,), (1,)), ((), ())), preferred_element_type=F32)


def dot_nn(a, b):
    return jnp.dot(a, b, preferred_element_type=F32)


def sign_table(hashes):
    buckets = lax.broadcasted_iota(jnp.int32, (SK, hashes.shape[1]), 0)
    signs = (1 - 2 * (hashes[1:2, :] & 1)).astype(F32)
    return jnp.where(buckets == hashes[0:1, :], signs, 0.0).astype(BF16)


def rem(value, count):
    return lax.rem(value + count, count)


class Place:
    def __init__(self):
        self.planes, self.chips, self.cores = SEQ_GRID
        self.ys, self.halves = HEAD_GRID
        self.width = self.chips * self.cores
        seq = lax.axis_index("seq")
        head = lax.axis_index("head")
        self.seq, self.head = seq, head
        self.i = lax.rem(seq, self.width)
        self.z = seq // self.width
        self.c = lax.rem(self.i, self.cores)
        self.x = self.i // self.cores
        self.y = head // self.halves
        self.half = lax.rem(head, self.halves)

    def at(self, z=None, i=None, y=None, half=None):
        z = self.z if z is None else z
        i = self.i if i is None else i
        y = self.y if y is None else y
        half = self.half if half is None else half
        return (z * self.width + i, y * self.halves + half)


def remote(src, dst, send_sem, recv_sem, device):
    return pltpu.make_async_remote_copy(
        src_ref=src, dst_ref=dst, send_sem=send_sem, recv_sem=recv_sem, device_id=device, device_id_type=MESH
    )


def greet(devices):
    barrier = pltpu.get_barrier_semaphore()
    for device in devices:
        pl.semaphore_signal(barrier, inc=1, device_id=device, device_id_type=MESH)


def kernel(
    starts_ref, targets_ref, x_ref, q_ref, k_ref, v_ref, do_ref, xh_ref, qh_ref, kh_ref, vh_ref,
    out_ref,
    qall, kv, scores, wgrads, stat, kmt, stat_send, stat_recv, total, dq_acc, dkv_acc,
    dkv_send, dkv_recv, dq_send, dq_recv, iy, iz, grad_sum,
    products, near, plane_docs, far_send, far,
    inputs, starts, targets, input_hash, query_hash, key_hash, value_hash, input_sem, hello, q_recv, q_own, q_ring, q_sib, kv_send_sem, kv_recv_sem, pool, st_recv_sem,
    dkv_send_sem, dkv_recv_sem, dq_send_sem, dq_recv_sem, iy_send_sem, iy_recv_sem, iz_send_sem, iz_recv_sem,
    near_recv_sem, plane_recv_sem, far_recv_sem,
):
    me = Place()
    planes, chips, width = me.planes, me.chips, me.width
    x, c, z, i = me.x, me.c, me.z, me.i
    rows = 2 * T
    scale = 1.0 / math.sqrt(F)
    scale2 = scale * math.log2(math.e)

    ys, halves = me.ys, me.halves
    place_in_group = lax.rem(i, GROUP)
    group_first = i - place_in_group
    near_peers = []
    for o in range(1, GROUP * ys):
        near_peers.append((rem(place_in_group + o // ys, GROUP), rem(me.y + o % ys, ys)))
    far_peers = []
    for o in range(1, planes * halves):
        far_peers.append((rem(z + o // halves, planes), rem(me.half + o % halves, halves)))
    line = planes * halves

    def along(steps):
        to = rem(me.half * planes + z + steps, line)
        return me.at(z=lax.rem(to, planes), half=to // planes)

    friends = [along(o) for o in sorted({o % line for o in (1, 2, -1, -2)} - {0})]
    hellos = 3 if line > 5 else 0

    def pass_hello(n):
        for steps in (2, -2):
            pl.semaphore_signal(hello.at[n], inc=1, device_id=along(steps), device_id_type=MESH)

    def hear_hello(n):
        pl.semaphore_wait(hello.at[n], 2)

    friends += [me.at(y=rem(me.y + o, ys)) for o in range(1, ys)]
    friends += [me.at(i=rem(i + o, width)) for o in range(1, width)]
    greet(friends)

    mine = pl.ds(pl.multiple_of(c * T, T), T)
    loads = [pltpu.make_async_copy(k_ref, kv.at[z, 0], input_sem.at[0]), pltpu.make_async_copy(v_ref, kv.at[z, 1], input_sem.at[1])]
    for part, ref in enumerate((q_ref, do_ref)):
        for h in range(H):
            loads.append(
                pltpu.make_async_copy(
                    ref.at[:, pl.ds(h * F, F)], qall.at[x, part, h, mine, :], input_sem.at[2 + part * H + h]
                )
            )
    later = (
        (x_ref, inputs), (xh_ref, input_hash), (qh_ref, query_hash), (kh_ref, key_hash), (vh_ref, value_hash),
        (starts_ref, starts), (targets_ref, targets),
    )
    later_loads = [
        pltpu.make_async_copy(ref, place, input_sem.at[2 + 2 * H + n]) for n, (ref, place) in enumerate(later)
    ]
    for load in loads + later_loads:
        load.start()
    for load in loads:
        load.wait()

    def piece(step, core, part):
        s = rem(x + step, chips)
        ref = qall.at[s, part, :, pl.ds(pl.multiple_of(core * T, T), T), :]
        return ref, q_recv.at[s, core, part]

    def send_piece(step, core, part, send_sem, target):
        ref, recv_sem = piece(step, core, part)
        return remote(ref, ref, send_sem, recv_sem, target)

    sibling = me.at(i=x * 2 + 1 - c)
    right = me.at(i=rem(x + 1, chips) * 2 + c)
    left = me.at(i=rem(x + chips - 1, chips) * 2 + c)
    own_copies = [
        send_piece(0, c, part, q_own.at[n, part], target)
        for n, target in enumerate((sibling, right, left)) for part in range(2)
    ]
    ring_copies = [
        send_piece(chips - 1, c, 0, q_ring.at[0], right),
        send_piece(1, c, 1, q_ring.at[1], left),
    ]
    sib_copies = {
        (step, part): send_piece(step, c, part, q_sib.at[step - 1, part], sibling)
        for step in (1, 2, 3) for part in range(2)
    }

    def wait_piece(step, core, part):
        ref, recv_sem = piece(step, core, part)
        remote(ref, ref, q_own.at[0, 0], recv_sem, sibling).wait_recv()

    def kv_copy(b, hops, part):
        return remote(
            kv.at[b, part], kv.at[b, part], kv_send_sem.at[b // 2, hops - 1, part], kv_recv_sem.at[b, part],
            me.at(z=rem(z + hops, planes)),
        )

    def relay_kv(b, part):
        @pl.when(z + 2 < planes)
        def _():
            kv_copy(b, 2, part).start()

        @pl.when(z + 1 < planes)
        def _():
            kv_copy(b, 1, part).start()

    pl.semaphore_wait(pltpu.get_barrier_semaphore(), len(friends))

    for part in range(2):
        relay_kv(z, part)
    for target, part in ((1, 0), (2, 1), (0, 0), (0, 1), (1, 1), (2, 0)):
        own_copies[2 * target + part].start()

    if hellos:
        pass_hello(0)
    for load in later_loads:
        load.wait()

    input_part = dot_nt(sign_table(input_hash[...]), inputs[...])
    iy[me.y] = input_part.astype(BF16)
    query_table = sign_table(query_hash[...])
    query_tables = jnp.concatenate([query_table[:, h * F:(h + 1) * F] for h in range(H)], axis=0)
    key_table = sign_table(key_hash[...])
    value_table = sign_table(value_hash[...])
    for s in range(chips):
        stat[s, 0:1, :] = jnp.full((1, H * rows), LOW, F32)
        stat[s, 1:3, :] = jnp.zeros((2, H * rows), F32)
    dq_acc[...] = jnp.zeros_like(dq_acc)
    dkv_acc[...] = jnp.zeros_like(dkv_acc)
    grad_sum[3 * SK:, :] = jnp.zeros((SK, T), F32)

    doc_count = starts.shape[0]
    group_tokens = GROUP * T
    tokens = lax.broadcasted_iota(jnp.int32, (1, T), 1)
    here = tokens + me.seq * T
    here_group = (me.seq // GROUP) * group_tokens
    slot_group = (z * (width // GROUP) + tokens // (2 * GROUP)) * group_tokens
    doc_of = jnp.zeros((1, T), jnp.int32)
    slot_first = jnp.zeros((1, T), jnp.int32)
    slot_past = jnp.zeros((1, T), jnp.int32)
    for d in range(doc_count):
        begins = starts[d]
        doc_of = doc_of + jnp.where(jnp.logical_and(begins <= here, begins > here_group), 1, 0)
        slot_first = slot_first + jnp.where(begins < slot_group, 1, 0)
        slot_past = slot_past + jnp.where(begins < slot_group + group_tokens, 1, 0)
    slot_doc = slot_first + lax.rem(tokens, 2 * GROUP)
    slot_doc = jnp.where(slot_doc < slot_past, slot_doc, -1)
    slot_row = jnp.full((1, T), -1, jnp.int32)
    for d in range(doc_count):
        slot_row = jnp.where(slot_doc == d, targets[d], slot_row)

    iy_copies = [
        remote(iy.at[me.y], iy.at[me.y], iy_send_sem.at[o - 1], iy_recv_sem.at[me.y], me.at(y=rem(me.y + o, me.ys)))
        for o in range(1, me.ys)
    ]
    for copy in iy_copies:
        copy.start()
    iz_copy = remote(iz.at[me.half], iz.at[me.half], iz_send_sem.at[0], iz_recv_sem.at[me.half], me.at(half=1 - me.half))

    def input_over_y():
        for o in range(1, me.ys):
            y = rem(me.y + o, me.ys)
            remote(iy.at[y], iy.at[y], iy_send_sem.at[0], iy_recv_sem.at[y], me.at(y=y)).wait_recv()
        summed = iy[0].astype(F32)
        for y in range(1, me.ys):
            summed = summed + iy[y].astype(F32)
        iz[me.half] = summed.astype(BF16)

    block_pairs = z // 2 + 1

    def two_blocks(j, part):
        return jnp.concatenate([kv[z - 2 * j, part], kv[jnp.maximum(z - 2 * j - 1, 0), part]], axis=0)

    def first_unit(s, j, masked):
        keys, values = two_blocks(j, 0), two_blocks(j, 1)
        for h in range(H):
            cols = pl.ds(h * rows, rows)
            st = dot_nt(keys, qall[s, 0, h]) * scale2
            if masked:
                row = lax.broadcasted_iota(jnp.int32, (2 * T, rows), 0)
                near_place = jnp.where(j == 0, i * T, -T)
                far_place = jnp.where(2 * j + 1 <= z, -2 * T, rows * chips)
                query_place = lax.broadcasted_iota(jnp.int32, (2 * T, rows), 1) + s * rows
                st = jnp.where(row + jnp.where(row < T, near_place, far_place) <= query_place, st, LOW)
            dp = dot_nt(values, qall[s, 1, h])
            scores[s, j, :, cols] = st
            wgrads[s, j, :, cols] = dp
            old_top = stat[s, 0:1, cols]
            top = jnp.maximum(old_top, jnp.max(st, axis=0, keepdims=True))
            e = jnp.exp2(st - top)
            keep = jnp.exp2(old_top - top)
            stat[s, 0:1, cols] = top
            stat[s, 1:2, cols] = stat[s, 1:2, cols] * keep + jnp.sum(e, axis=0, keepdims=True)
            stat[s, 2:3, cols] = stat[s, 2:3, cols] * keep + jnp.sum(e * dp, axis=0, keepdims=True)

    def arrived_kv(t):
        for part in range(2):
            kv_copy(z - t, 1, part).wait_recv()

    def sketch_keys(j):
        kmt[j] = dot_nt(query_tables, two_blocks(j, 0)).astype(BF16)

    def first_blocks(s, low, high):
        def over_blocks(j, carry):
            bordering = jnp.logical_or(j == 0, 2 * j == z)

            @pl.when(bordering)
            def _():
                first_unit(s, j, True)

            @pl.when(jnp.logical_not(bordering))
            def _():
                first_unit(s, j, False)

            return carry

        lax.fori_loop(low, high, over_blocks, 0)

    def even_arrival(t):
        @pl.when(t <= z)
        def _():
            for part in range(2):
                kv_copy(z - t, 1, part).wait_recv()
                relay_kv(z - t, part)

    def odd_arrival(t):
        @pl.when(t <= z)
        def _():
            arrived_kv(t)

        @pl.when(t // 2 < block_pairs)
        def _():
            sketch_keys(t // 2)

    def hand_on(step, part):
        wait_piece(step, c, part)
        sib_copies[(step, part)].start()

    pairs = chips // 2

    def stat_copies(g):
        return [
            remote(
                stat_send.at[g], stat_recv.at[g, i], pool.at[g * width + o - 1], st_recv_sem.at[g, i],
                me.at(i=rem(i + o, width)),
            )
            for o in range(1, width)
        ]

    def first_step(n, carry):
        @pl.when(n == 0)
        def _():
            even_arrival(2)
            for n, (step, part) in enumerate(((chips - 1, 0), (1, 1))):
                wait_piece(step, c, part)
                ring_copies[n].start()
                sib_copies[(step, part)].start()
            odd_arrival(1)
            for part in range(2):
                wait_piece(0, 1 - c, part)

        @pl.when(n == 1)
        def _():
            even_arrival(4)
            hand_on(chips - 1, 1)
            hand_on(1, 0)
            if hellos:
                hear_hello(0)
                pass_hello(1)
            odd_arrival(3)

        @pl.when(n == 2)
        def _():
            for step in (chips - 1, 1):
                for part in range(2):
                    wait_piece(step, 1 - c, part)
            input_over_y()

        @pl.when(n == 3)
        def _():
            hand_on(2, 0)
            hand_on(2, 1)
            even_arrival(6)
            if hellos:
                hear_hello(1)
                pass_hello(2)

        @pl.when(n == 4)
        def _():
            odd_arrival(5)

        @pl.when(n == 7)
        def _():
            odd_arrival(7)
            for part in range(2):
                wait_piece(2, 1 - c, part)

        s = jnp.where(n < 2, x, jnp.where(n == 2, x + 1, jnp.where(n == 3, x + chips - 1, x + n - 5)))
        s = jnp.where(n < 7, rem(s, chips), n - 7)
        low = jnp.where(n < 2, n, jnp.where(n < 4, 0, jnp.where(n < 7, 2, jnp.where(s == rem(x + 2, chips), 0, 3))))
        high = jnp.where(n < 2, n + 1, jnp.where(n < 4, 2, jnp.where(n < 7, 3, 4)))
        first_blocks(s, low, jnp.minimum(high, block_pairs))

        @pl.when(jnp.logical_or(n == 8, n == 10))
        def _():
            g = (n - 8) // 2
            for m in range(2):
                stat_send[g, 3 * m:3 * m + 3, :] = stat[2 * g + m, 0:3, :]
            for copy in stat_copies(g):
                copy.start()
            stat_recv[g, i] = stat_send[g]

        return carry

    lax.fori_loop(0, 11, first_step, 0)
    if hellos:
        hear_hello(2)
    if me.halves > 1:
        iz_copy.start()

    def add_statistics(g):
        for o in range(1, width):
            p = rem(i + o, width)
            remote(
                stat_send.at[g], stat_recv.at[g, p], pool.at[0], st_recv_sem.at[g, p], me.at(i=p)
            ).wait_recv()
        for n in range(2):
            first = 3 * n
            top = stat_recv[g, 0, first:first + 1, :]
            for p in range(1, width):
                top = jnp.maximum(top, stat_recv[g, p, first:first + 1, :])
            weight_sum = jnp.zeros_like(top)
            delta_sum = jnp.zeros_like(top)
            for p in range(width):
                factor = jnp.exp2(stat_recv[g, p, first:first + 1, :] - top)
                weight_sum = weight_sum + stat_recv[g, p, first + 1:first + 2, :] * factor
                delta_sum = delta_sum + stat_recv[g, p, first + 2:first + 3, :] * factor
            total[2 * g + n, 0:1, :] = top + jnp.log2(weight_sum)
            total[2 * g + n, 1:2, :] = delta_sum / weight_sum

    def second_unit(s, j):
        lows, grads = [], []
        for h in range(H):
            cols = pl.ds(h * rows, rows)
            p = jnp.exp2(scores[s, j, :, cols] - total[s, 0:1, cols])
            g = p * (wgrads[s, j, :, cols] - total[s, 1:2, cols])
            lows.append(p.astype(BF16))
            g = g.astype(BF16)
            grads.append(g)
            dq_acc[s] += dot_nn(kmt[j, h * SK:(h + 1) * SK, :], g)
        low = jnp.concatenate(lows, axis=1)
        grad = jnp.concatenate(grads, axis=1)
        dkv_acc[j, 0] += dot_nn(grad, qall[s, 0].reshape(H * rows, F))
        dkv_acc[j, 1] += dot_nn(low, qall[s, 1].reshape(H * rows, F))

    def dkv_copy(k, b):
        return remote(dkv_send.at[k], dkv_recv.at[z], dkv_send_sem.at[k], dkv_recv_sem.at[z], me.at(z=b))

    def send_dq(g):
        for s in (2 * g, 2 * g + 1):
            for core in range(2):
                dq_send[s * 2 + core] = (dq_acc[s, :, core * T:(core + 1) * T] * scale).astype(BF16)
        for n in range(GROUP):
            p = GROUP * g + n

            @pl.when(p != i)
            def _():
                dq_copy(p).start()

    def dq_copy(p):
        return remote(dq_send.at[p], dq_recv.at[i], dq_send_sem.at[p], dq_recv_sem.at[i], me.at(i=p))

    near_pairs = (block_pairs + 1) // 2
    def second_step(m, carry):
        n = m - near_pairs
        j = jnp.where(n < 0, m, block_pairs - 1 - n)

        @pl.when(m == 0)
        def _():
            add_statistics(0)

        @pl.when(n == 0)
        def _():
            add_statistics(1)

        @pl.when(n == block_pairs - near_pairs)
        def _():
            send_dq(0)

        def over_chips(s, carry):
            second_unit(s, j)
            return carry

        first = jnp.where(n < 0, 0, jnp.where(j < near_pairs, 2, 0))
        lax.fori_loop(first, jnp.where(n < 0, 2, chips), over_chips, 0)

        @pl.when(n >= 0)
        def _():
            key_part = dot_nt(key_table, (dkv_acc[j, 0] * scale).astype(BF16)).astype(BF16)
            value_part = dot_nt(value_table, dkv_acc[j, 1].astype(BF16)).astype(BF16)
            for b in range(2):
                dkv_send[2 * j + b, 0:SK, :] = key_part[:, b * T:(b + 1) * T]
                dkv_send[2 * j + b, SK:, :] = value_part[:, b * T:(b + 1) * T]

        @pl.when(jnp.logical_and(n >= 0, 2 * j + 1 <= z))
        def _():
            dkv_copy(2 * j + 1, z - 2 * j - 1).start()

        @pl.when(jnp.logical_and(n >= 0, j > 0))
        def _():
            dkv_copy(2 * j, z - 2 * j).start()

        return carry

    lax.fori_loop(0, near_pairs + block_pairs, second_step, 0)
    send_dq(1)

    for copy in own_copies + ring_copies + list(sib_copies.values()) + iy_copies:
        copy.wait_send()
    if me.halves > 1:
        iz_copy.wait_send()

    for g in range(pairs):
        for copy in stat_copies(g):
            copy.wait_send()
    for p in range(width):
        @pl.when(p != i)
        def _():
            dq_copy(p).wait_send()

    def left_kv(n, carry):
        b = z - 2 * n

        for part in range(2):
            @pl.when(z + 2 < planes)
            def _():
                kv_copy(b, 2, part).wait_send()

            @pl.when(z + 1 < planes)
            def _():
                kv_copy(b, 1, part).wait_send()

        return carry

    lax.fori_loop(0, z // 2 + 1, left_kv, 0)

    def left_dkv(k, carry):
        dkv_copy(k, z - k).wait_send()
        return carry

    lax.fori_loop(1, z + 1, left_dkv, 0)

    if me.halves > 1:
        away = 1 - me.half
        remote(iz.at[away], iz.at[away], iz_send_sem.at[0], iz_recv_sem.at[away], me.at(half=away)).wait_recv()
    summed = iz[0].astype(F32)
    for half in range(1, me.halves):
        summed = summed + iz[half].astype(F32)
    input_sketch = summed * math.sqrt(SK / (x_ref.shape[1] * ys * halves))

    heads = me.ys * me.halves
    kv_factor = math.sqrt(SK / (F * heads))
    grad_sum[SK:3 * SK, :] = dkv_send[0].astype(F32) * kv_factor

    def add_kv(b, carry):
        remote(dkv_send.at[0], dkv_recv.at[b], dkv_send_sem.at[0], dkv_recv_sem.at[b], me.at(z=rem(z + 1, planes))).wait_recv()
        grad_sum[SK:3 * SK, :] += dkv_recv[b].astype(F32) * kv_factor
        return carry

    dq_recv[i] = dq_send[i]
    lax.fori_loop(z + 1, planes, add_kv, 0)
    for o in range(1, width):
        p = rem(i + o, width)
        remote(dq_send.at[p], dq_recv.at[p], dq_send_sem.at[0], dq_recv_sem.at[p], me.at(i=p)).wait_recv()
    query_sum = dq_recv[0].astype(F32)
    for p in range(1, width):
        query_sum = query_sum + dq_recv[p].astype(F32)
    grad_sum[0:SK, :] = query_sum * math.sqrt(SK / (H * F * heads))

    band = SK // ys
    masked = jnp.concatenate([jnp.where(doc_of == e, input_sketch, 0.0) for e in range(DOCS_MOST)], axis=0)
    grads = grad_sum[...]
    masked_high = masked.astype(BF16)
    masked_low = (masked - masked_high.astype(F32)).astype(BF16)
    grads_high = grads.astype(BF16)
    grads_low = (grads - grads_high.astype(F32)).astype(BF16)
    product = dot_nt(masked_high, grads_high) + (dot_nt(masked_high, grads_low) + dot_nt(masked_low, grads_high))
    product = product.reshape(DOCS_MOST // 2, 2, SK, 4 * SK)
    products[:, 0:2] = product[:, :, :, 0:2 * SK].astype(BF16)
    value_product = product[:, :, :, 2 * SK:]
    moved = pltpu.roll(value_product[:, 1].reshape(DOCS_MOST // 2 * SK, 2 * SK), SK, 1)
    products[:, 2] = (value_product[:, 0] + moved.reshape(DOCS_MOST // 2, SK, 2 * SK)).astype(BF16)

    def part(p, y):
        return products.at[p, :, pl.ds(pl.multiple_of(y * band, band), band), :]

    my_slot = place_in_group * ys + me.y
    near_copies = [
        remote(part(p, y), near.at[my_slot], pool.at[n], near_recv_sem.at[my_slot], me.at(i=group_first + p, y=y))
        for n, (p, y) in enumerate(near_peers)
    ]
    for copy in near_copies:
        copy.start()
    summed = part(place_in_group, me.y)[...].astype(F32)
    for p, y in near_peers:
        slot = p * ys + y
        remote(near.at[slot], near.at[slot], pool.at[0], near_recv_sem.at[slot], me.at(i=group_first + p, y=y)).wait_recv()
        summed = summed + near[slot].astype(F32)
    plane_docs[i] = summed.astype(BF16)

    plane_copies = [
        remote(plane_docs.at[i], plane_docs.at[i], dq_send_sem.at[o - 1], plane_recv_sem.at[i], me.at(i=rem(i + o, width)))
        for o in range(1, width)
    ]
    for copy in plane_copies:
        copy.start()
    for o in range(1, width):
        p = rem(i + o, width)
        remote(plane_docs.at[p], plane_docs.at[p], dq_send_sem.at[0], plane_recv_sem.at[p], me.at(i=p)).wait_recv()

    for copy in near_copies:
        copy.wait_send()

    my_line = z * halves + me.half
    own = band // halves

    def far_copy(fz, half):
        slot = fz * halves + half
        return remote(far_send.at[slot], far.at[my_line], pool.at[slot], far_recv_sem.at[my_line], me.at(z=fz, half=half))

    def gather_row(n, carry):
        fz = rem(z + n, planes)
        row = fz * width + i
        found = jnp.zeros((band, 2 * SK), F32)
        values = [jnp.zeros((band, 2 * SK), F32)] * 2
        for j in range(width):
            for e in range(2):
                chosen = jnp.broadcast_to(slot_row[:, 2 * j + e:2 * j + e + 1], (band, 2 * SK)) == row
                found = found + jnp.where(chosen, plane_docs[j, e].astype(F32), 0.0)
                values[e] = values[e] + jnp.where(chosen, plane_docs[j, 2].astype(F32), 0.0)
        lanes = lax.broadcasted_iota(jnp.int32, (band, 2 * SK), 1)
        value_rows = jnp.where(lanes < SK, values[0] + pltpu.roll(values[1], SK, 1), 0.0)
        for half in range(halves):
            mine_of = slice(half * own, (half + 1) * own)
            both = jnp.concatenate([found[mine_of], value_rows[mine_of]], axis=0)
            far_send[fz * halves + half] = both.astype(BF16)

            @pl.when(jnp.logical_or(fz != z, me.half != half))
            def _():
                far_copy(fz, half).start()

        return carry

    lax.fori_loop(0, planes, gather_row, 0)
    for copy in plane_copies:
        copy.wait_send()
    result = far_send[my_line].astype(F32)
    for fz, half in far_peers:
        slot = fz * halves + half
        remote(far.at[slot], far.at[slot], pool.at[0], far_recv_sem.at[slot], me.at(z=fz, half=half)).wait_recv()
        result = result + far[slot].astype(F32)
    query_key, value_only = result[0:own], result[own:]
    key_query, moved_value = pltpu.roll(query_key, SK, 1), pltpu.roll(value_only, SK, 1)
    first_half = lax.broadcasted_iota(jnp.int32, (1, 2 * SK), 1) < SK
    for p, (even, odd) in enumerate(((query_key, key_query), (key_query, query_key), (value_only, moved_value))):
        for pair in range(own // 2):
            out_ref[0, p:p + 1, pair * 2 * SK:(pair + 1) * 2 * SK] = jnp.where(
                first_half, even[2 * pair:2 * pair + 1], odd[2 * pair + 1:2 * pair + 2]
            )
    for fz, half in far_peers:
        far_copy(fz, half).wait_send()


def sketches_of(
    doc_starts, doc_rows, layer_input, queries, key_states, value_states, out_grad,
    input_hash, query_hash, key_hash, value_hash,
):
    planes, chips, cores = SEQ_GRID
    ys, halves = HEAD_GRID
    width = chips * cores
    rows = 2 * T
    line = planes * halves
    band = SK // ys
    pairs = chips // 2
    dma = pltpu.SemaphoreType.DMA
    vmem = pltpu.VMEM
    return pl.pallas_call(
        kernel,
        out_shape=jax.ShapeDtypeStruct((1, 3, band // halves * SK), F32),
        in_specs=[pl.BlockSpec(memory_space=pl.ANY)] * 11,
        out_specs=pl.BlockSpec(memory_space=pltpu.VMEM),
        scratch_shapes=[
            vmem((chips, 2, H, rows, F), BF16),
            vmem((planes, 2, T, F), BF16),
            vmem((chips, planes // 2, 2 * T, H * rows), F32),
            vmem((chips, planes // 2, 2 * T, H * rows), F32),
            vmem((chips, 8, H * rows), F32),
            vmem((planes // 2, H * SK, 2 * T), BF16),
            vmem((pairs, 8, H * rows), F32),
            vmem((pairs, width, 8, H * rows), F32),
            vmem((chips, 8, H * rows), F32),
            vmem((chips, SK, rows), F32),
            vmem((planes // 2, 2, 2 * T, F), F32),
            vmem((planes, 2 * SK, T), BF16),
            vmem((planes, 2 * SK, T), BF16),
            vmem((width, SK, T), BF16),
            vmem((width, SK, T), BF16),
            vmem((ys, SK, T), BF16),
            vmem((halves, SK, T), BF16),
            vmem((4 * SK, T), F32),
            vmem((DOCS_MOST // 2, 3, SK, 2 * SK), BF16),
            vmem((GROUP * ys, 3, band, 2 * SK), BF16),
            vmem((width, 3, band, 2 * SK), BF16),
            vmem((line, 2 * band // halves, 2 * SK), BF16),
            vmem((line, 2 * band // halves, 2 * SK), BF16),
            vmem(layer_input.shape, BF16),
            pltpu.SMEM(doc_starts.shape, jnp.int32), pltpu.SMEM(doc_rows.shape, jnp.int32),
            vmem(input_hash.shape, jnp.int32), vmem(query_hash.shape, jnp.int32),
            vmem(key_hash.shape, jnp.int32), vmem(value_hash.shape, jnp.int32),
            dma((2 + 2 * H + 7,)), pltpu.SemaphoreType.REGULAR((3,)),
            dma((chips, 2, 2)), dma((3, 2)), dma((2,)), dma((3, 2)),
            dma(((planes + 1) // 2, 2, 2)), dma((planes, 2)),
            dma((max(pairs * width, GROUP * ys, line),)), dma((pairs, width)),
            dma((planes,)), dma((planes,)),
            dma((width,)), dma((width,)),
            dma((ys,)), dma((ys,)), dma((halves,)), dma((halves,)),
            dma((GROUP * ys,)), dma((width,)), dma((line,)),
        ],
        compiler_params=pltpu.CompilerParams(
            collective_id=0, has_side_effects=True, vmem_limit_bytes=56 * 1024 * 1024
        ),
        name="sketches",
    )(
        doc_starts, doc_rows, layer_input, queries, key_states, value_states, out_grad,
        input_hash, query_hash, key_hash, value_hash,
    )


def on_device(
    layer_input, queries, key_states, value_states, out_grad,
    input_hash, query_hash, key_hash, value_hash, doc_starts, doc_rows,
):
    return sketches_of(
        doc_starts, doc_rows, layer_input, queries, key_states, value_states, out_grad,
        input_hash, query_hash, key_hash, value_hash,
    )


def solution(mesh):
    return jax.shard_map(
        on_device,
        mesh=mesh,
        in_specs=(
            P("seq", "head"), P("seq", "head"), P("seq", "head"), P("seq", "head"), P("seq", "head"),
            P(None, "head"), P(None, "head"), P(None, "head"), P(None, "head"),
            P(), P(),
        ),
        out_specs=P("seq", None, "head"),
        check_vma=False,
    )
```

```python
import functools
import math

import jax
import jax.numpy as jnp
from jax import lax
from jax.experimental import pallas as pl
from jax.experimental.pallas import tpu as pltpu
from jax.sharding import PartitionSpec as P

SEQ_GRID = (8, 4, 2)
HEAD_GRID = (4, 2)

T = 128
F = 128
H = 4
SK = 64
GROUP = 4
DOCS_MOST = 8
LOW = -1e30
MESH = pl.DeviceIdType.MESH
F32 = jnp.float32
BF16 = jnp.bfloat16


def dot_nt(a, b):
    return lax.dot_general(a, b, (((1,), (1,)), ((), ())), preferred_element_type=F32)


def dot_nn(a, b):
    return jnp.dot(a, b, preferred_element_type=F32)


def sign_table(hashes):
    buckets = lax.broadcasted_iota(jnp.int32, (SK, hashes.shape[1]), 0)
    signs = (1 - 2 * (hashes[1:2, :] & 1)).astype(F32)
    return jnp.where(buckets == hashes[0:1, :], signs, 0.0).astype(BF16)


def rem(value, count):
    return lax.rem(value + count, count)


def far_first(count):
    return sorted(range(1, count), key=lambda o: -min(o, count - o))


class Place:
    def __init__(self):
        self.planes, self.chips, self.cores = SEQ_GRID
        self.ys, self.halves = HEAD_GRID
        self.width = self.chips * self.cores
        seq = lax.axis_index("seq")
        head = lax.axis_index("head")
        self.seq, self.head = seq, head
        self.i = lax.rem(seq, self.width)
        self.z = seq // self.width
        self.c = lax.rem(self.i, self.cores)
        self.x = self.i // self.cores
        self.y = head // self.halves
        self.half = lax.rem(head, self.halves)

    def at(self, z=None, i=None, y=None, half=None):
        z = self.z if z is None else z
        i = self.i if i is None else i
        y = self.y if y is None else y
        half = self.half if half is None else half
        return (z * self.width + i, y * self.halves + half)


def remote(src, dst, send_sem, recv_sem, device):
    return pltpu.make_async_remote_copy(
        src_ref=src, dst_ref=dst, send_sem=send_sem, recv_sem=recv_sem, device_id=device, device_id_type=MESH
    )


def greet(devices):
    barrier = pltpu.get_barrier_semaphore()
    for device in devices:
        pl.semaphore_signal(barrier, inc=1, device_id=device, device_id_type=MESH)


def kernel(
    starts_ref, targets_ref, x_ref, q_ref, k_ref, v_ref, do_ref, xh_ref, qh_ref, kh_ref, vh_ref,
    out_ref,
    qall, kv, scores, wgrads, stat, kmt, stat_send, stat_recv, total, dq_acc, dkv_acc,
    dkv_send, dkv_recv, dq_send, dq_recv, iy, iz, grad_sum,
    products, near, plane_docs, doc_target, far_send, far,
    inputs, starts, targets, input_hash, query_hash, key_hash, value_hash, input_sem, hello, q_recv, q_own, q_ring, q_sib, kv_send_sem, kv_recv_sem, pool, st_recv_sem,
    dkv_send_sem, dkv_recv_sem, dq_send_sem, dq_recv_sem, iy_send_sem, iy_recv_sem, iz_send_sem, iz_recv_sem,
    near_recv_sem, plane_recv_sem, far_recv_sem,
):
    me = Place()
    planes, chips, width = me.planes, me.chips, me.width
    x, c, z, i = me.x, me.c, me.z, me.i
    rows = 2 * T
    scale = 1.0 / math.sqrt(F)
    scale2 = scale * math.log2(math.e)

    ys, halves = me.ys, me.halves
    place_in_group = lax.rem(i, GROUP)
    group_first = i - place_in_group
    near_peers = []
    for p in far_first(GROUP) + [0]:
        for y in far_first(ys) + [0]:
            if (p, y) != (0, 0):
                near_peers.append((rem(place_in_group + p, GROUP), rem(me.y + y, ys)))
    far_peers = []
    for o in range(1, planes * halves):
        far_peers.append((rem(z + o // halves, planes), rem(me.half + o % halves, halves)))
    line = planes * halves

    def along(steps):
        to = rem(me.half * planes + z + steps, line)
        return me.at(z=lax.rem(to, planes), half=to // planes)

    friends = [along(o) for o in sorted({o % line for o in (1, 2, -1, -2)} - {0})]
    hellos = 3 if line > 5 else 0

    def pass_hello(n):
        for steps in (2, -2):
            pl.semaphore_signal(hello.at[n], inc=1, device_id=along(steps), device_id_type=MESH)

    def hear_hello(n):
        pl.semaphore_wait(hello.at[n], 2)

    friends += [me.at(y=rem(me.y + o, ys)) for o in range(1, ys)]
    friends += [me.at(i=rem(i + o, width)) for o in far_first(width)]
    greet(friends)

    mine = pl.ds(pl.multiple_of(c * T, T), T)
    loads = [pltpu.make_async_copy(k_ref, kv.at[z, 0], input_sem.at[0]), pltpu.make_async_copy(v_ref, kv.at[z, 1], input_sem.at[1])]
    for part, ref in enumerate((q_ref, do_ref)):
        for h in range(H):
            loads.append(
                pltpu.make_async_copy(
                    ref.at[:, pl.ds(h * F, F)], qall.at[x, part, h, mine, :], input_sem.at[2 + part * H + h]
                )
            )
    later = (
        (x_ref, inputs), (xh_ref, input_hash), (qh_ref, query_hash), (kh_ref, key_hash), (vh_ref, value_hash),
        (starts_ref, starts), (targets_ref, targets),
    )
    later_loads = [
        pltpu.make_async_copy(ref, place, input_sem.at[2 + 2 * H + n]) for n, (ref, place) in enumerate(later)
    ]
    for load in loads + later_loads:
        load.start()
    for load in loads:
        load.wait()

    def piece(step, core, part):
        s = rem(x + step, chips)
        ref = qall.at[s, part, :, pl.ds(pl.multiple_of(core * T, T), T), :]
        return ref, q_recv.at[s, core, part]

    def send_piece(step, core, part, send_sem, target):
        ref, recv_sem = piece(step, core, part)
        return remote(ref, ref, send_sem, recv_sem, target)

    sibling = me.at(i=x * 2 + 1 - c)
    right = me.at(i=rem(x + 1, chips) * 2 + c)
    left = me.at(i=rem(x + chips - 1, chips) * 2 + c)
    own_copies = [
        send_piece(0, c, part, q_own.at[n, part], target)
        for n, target in enumerate((sibling, right, left)) for part in range(2)
    ]
    ring_copies = [
        send_piece(chips - 1, c, 0, q_ring.at[0], right),
        send_piece(1, c, 1, q_ring.at[1], left),
    ]
    sib_copies = {
        (step, part): send_piece(step, c, part, q_sib.at[step - 1, part], sibling)
        for step in (1, 2, 3) for part in range(2)
    }

    def wait_piece(step, core, part):
        ref, recv_sem = piece(step, core, part)
        remote(ref, ref, q_own.at[0, 0], recv_sem, sibling).wait_recv()

    def kv_copy(b, hops, part):
        return remote(
            kv.at[b, part], kv.at[b, part], kv_send_sem.at[b // 2, hops - 1, part], kv_recv_sem.at[b, part],
            me.at(z=rem(z + hops, planes)),
        )

    def relay_kv(b, part):
        @pl.when(z + 2 < planes)
        def _():
            kv_copy(b, 2, part).start()

        @pl.when(z + 1 < planes)
        def _():
            kv_copy(b, 1, part).start()

    pl.semaphore_wait(pltpu.get_barrier_semaphore(), len(friends))

    for part in range(2):
        relay_kv(z, part)
    for target, part in ((1, 0), (2, 1), (0, 0), (0, 1), (1, 1), (2, 0)):
        own_copies[2 * target + part].start()

    if hellos:
        pass_hello(0)
    for load in later_loads:
        load.wait()

    input_part = dot_nt(sign_table(input_hash[...]), inputs[...])
    iy[me.y] = input_part.astype(BF16)
    query_table = sign_table(query_hash[...])
    query_tables = jnp.concatenate([query_table[:, h * F:(h + 1) * F] for h in range(H)], axis=0)
    key_table = sign_table(key_hash[...])
    value_table = sign_table(value_hash[...])
    for s in range(chips):
        stat[s, 0:1, :] = jnp.full((1, H * rows), LOW, F32)
        stat[s, 1:3, :] = jnp.zeros((2, H * rows), F32)
    dq_acc[...] = jnp.zeros_like(dq_acc)
    dkv_acc[...] = jnp.zeros_like(dkv_acc)
    grad_sum[3 * SK:, :] = jnp.zeros((SK, T), F32)

    doc_count = starts.shape[0]
    group_tokens = GROUP * T
    tokens = lax.broadcasted_iota(jnp.int32, (1, T), 1)
    here = tokens + me.seq * T
    here_group = (me.seq // GROUP) * group_tokens
    slot_group = (z * (width // GROUP) + tokens // (2 * GROUP)) * group_tokens
    doc_of = jnp.zeros((1, T), jnp.int32)
    slot_first = jnp.zeros((1, T), jnp.int32)
    slot_past = jnp.zeros((1, T), jnp.int32)
    for d in range(doc_count):
        begins = starts[d]
        doc_of = doc_of + jnp.where(jnp.logical_and(begins <= here, begins > here_group), 1, 0)
        slot_first = slot_first + jnp.where(begins < slot_group, 1, 0)
        slot_past = slot_past + jnp.where(begins < slot_group + group_tokens, 1, 0)
    slot_doc = slot_first + lax.rem(tokens, 2 * GROUP)
    slot_doc = jnp.where(slot_doc < slot_past, slot_doc, -1)
    slot_row = jnp.full((1, T), -1, jnp.int32)
    for d in range(doc_count):
        slot_row = jnp.where(slot_doc == d, targets[d], slot_row)
    for n in range(2 * width):
        doc_target[n] = jnp.broadcast_to(slot_row[:, n:n + 1], doc_target.shape[1:])

    iy_copies = [
        remote(iy.at[me.y], iy.at[me.y], iy_send_sem.at[o - 1], iy_recv_sem.at[me.y], me.at(y=rem(me.y + o, me.ys)))
        for o in range(1, me.ys)
    ]
    for copy in iy_copies:
        copy.start()
    iz_copy = remote(iz.at[me.half], iz.at[me.half], iz_send_sem.at[0], iz_recv_sem.at[me.half], me.at(half=1 - me.half))

    def input_over_y():
        for o in range(1, me.ys):
            y = rem(me.y + o, me.ys)
            remote(iy.at[y], iy.at[y], iy_send_sem.at[0], iy_recv_sem.at[y], me.at(y=y)).wait_recv()
        summed = iy[0].astype(F32)
        for y in range(1, me.ys):
            summed = summed + iy[y].astype(F32)
        iz[me.half] = summed.astype(BF16)

    block_pairs = z // 2 + 1

    def two_blocks(j, part):
        return jnp.concatenate([kv[z - 2 * j, part], kv[jnp.maximum(z - 2 * j - 1, 0), part]], axis=0)

    def first_unit(s, j, masked):
        keys, values = two_blocks(j, 0), two_blocks(j, 1)
        for h in range(H):
            cols = pl.ds(h * rows, rows)
            st = dot_nt(keys, qall[s, 0, h]) * scale2
            if masked:
                row = lax.broadcasted_iota(jnp.int32, (2 * T, rows), 0)
                near_place = jnp.where(j == 0, i * T, -T)
                far_place = jnp.where(2 * j + 1 <= z, -2 * T, rows * chips)
                query_place = lax.broadcasted_iota(jnp.int32, (2 * T, rows), 1) + s * rows
                st = jnp.where(row + jnp.where(row < T, near_place, far_place) <= query_place, st, LOW)
            dp = dot_nt(values, qall[s, 1, h])
            scores[s, j, :, cols] = st
            wgrads[s, j, :, cols] = dp
            old_top = stat[s, 0:1, cols]
            top = jnp.maximum(old_top, jnp.max(st, axis=0, keepdims=True))
            e = jnp.exp2(st - top)
            keep = jnp.exp2(old_top - top)
            stat[s, 0:1, cols] = top
            stat[s, 1:2, cols] = stat[s, 1:2, cols] * keep + jnp.sum(e, axis=0, keepdims=True)
            stat[s, 2:3, cols] = stat[s, 2:3, cols] * keep + jnp.sum(e * dp, axis=0, keepdims=True)

    def arrived_kv(t):
        for part in range(2):
            kv_copy(z - t, 1, part).wait_recv()

    def sketch_keys(j):
        kmt[j] = dot_nt(query_tables, two_blocks(j, 0)).astype(BF16)

    def first_blocks(s, low, high):
        def over_blocks(j, carry):
            bordering = jnp.logical_or(j == 0, 2 * j == z)

            @pl.when(bordering)
            def _():
                first_unit(s, j, True)

            @pl.when(jnp.logical_not(bordering))
            def _():
                first_unit(s, j, False)

            return carry

        lax.fori_loop(low, high, over_blocks, 0)

    def even_arrival(t):
        @pl.when(t <= z)
        def _():
            for part in range(2):
                kv_copy(z - t, 1, part).wait_recv()
                relay_kv(z - t, part)

    def odd_arrival(t):
        @pl.when(t <= z)
        def _():
            arrived_kv(t)

        @pl.when(t // 2 < block_pairs)
        def _():
            sketch_keys(t // 2)

    def hand_on(step, part):
        wait_piece(step, c, part)
        sib_copies[(step, part)].start()

    pairs = chips // 2

    def stat_copies(g):
        return [
            remote(
                stat_send.at[g], stat_recv.at[g, i], pool.at[g * width + o - 1], st_recv_sem.at[g, i],
                me.at(i=rem(i + o, width)),
            )
            for o in far_first(width)
        ]

    def first_step(n, carry):
        @pl.when(n == 0)
        def _():
            even_arrival(2)
            for n, (step, part) in enumerate(((chips - 1, 0), (1, 1))):
                wait_piece(step, c, part)
                ring_copies[n].start()
                sib_copies[(step, part)].start()
            odd_arrival(1)
            for part in range(2):
                wait_piece(0, 1 - c, part)

        @pl.when(n == 1)
        def _():
            even_arrival(4)
            hand_on(chips - 1, 1)
            hand_on(1, 0)
            if hellos:
                hear_hello(0)
                pass_hello(1)
            odd_arrival(3)

        @pl.when(n == 2)
        def _():
            for step in (chips - 1, 1):
                for part in range(2):
                    wait_piece(step, 1 - c, part)
            input_over_y()

        @pl.when(n == 3)
        def _():
            hand_on(2, 0)
            hand_on(2, 1)
            even_arrival(6)
            if hellos:
                hear_hello(1)
                pass_hello(2)

        @pl.when(n == 4)
        def _():
            odd_arrival(5)

        @pl.when(n == 7)
        def _():
            odd_arrival(7)
            for part in range(2):
                wait_piece(2, 1 - c, part)

        s = jnp.where(n < 2, x, jnp.where(n == 2, x + 1, jnp.where(n == 3, x + chips - 1, x + n - 5)))
        s = jnp.where(n < 7, rem(s, chips), n - 7)
        low = jnp.where(n < 2, n, jnp.where(n < 4, 0, jnp.where(n < 7, 2, jnp.where(s == rem(x + 2, chips), 0, 3))))
        high = jnp.where(n < 2, n + 1, jnp.where(n < 4, 2, jnp.where(n < 7, 3, 4)))
        first_blocks(s, low, jnp.minimum(high, block_pairs))

        @pl.when(jnp.logical_or(n == 8, n == 10))
        def _():
            g = (n - 8) // 2
            for m in range(2):
                stat_send[g, 3 * m:3 * m + 3, :] = stat[2 * g + m, 0:3, :]
            for copy in stat_copies(g):
                copy.start()
            stat_recv[g, i] = stat_send[g]

        return carry

    lax.fori_loop(0, 11, first_step, 0)
    if hellos:
        hear_hello(2)
    if me.halves > 1:
        iz_copy.start()

    def add_statistics(g):
        for o in far_first(width):
            p = rem(i + o, width)
            remote(
                stat_send.at[g], stat_recv.at[g, p], pool.at[0], st_recv_sem.at[g, p], me.at(i=p)
            ).wait_recv()
        for n in range(2):
            first = 3 * n
            top = stat_recv[g, 0, first:first + 1, :]
            for p in range(1, width):
                top = jnp.maximum(top, stat_recv[g, p, first:first + 1, :])
            weight_sum = jnp.zeros_like(top)
            delta_sum = jnp.zeros_like(top)
            for p in range(width):
                factor = jnp.exp2(stat_recv[g, p, first:first + 1, :] - top)
                weight_sum = weight_sum + stat_recv[g, p, first + 1:first + 2, :] * factor
                delta_sum = delta_sum + stat_recv[g, p, first + 2:first + 3, :] * factor
            total[2 * g + n, 0:1, :] = top + jnp.log2(weight_sum)
            total[2 * g + n, 1:2, :] = delta_sum / weight_sum

    def second_unit(s, j):
        lows, grads = [], []
        for h in range(H):
            cols = pl.ds(h * rows, rows)
            p = jnp.exp2(scores[s, j, :, cols] - total[s, 0:1, cols])
            g = p * (wgrads[s, j, :, cols] - total[s, 1:2, cols])
            lows.append(p.astype(BF16))
            g = g.astype(BF16)
            grads.append(g)
            dq_acc[s] += dot_nn(kmt[j, h * SK:(h + 1) * SK, :], g)
        low = jnp.concatenate(lows, axis=1)
        grad = jnp.concatenate(grads, axis=1)
        dkv_acc[j, 0] += dot_nn(grad, qall[s, 0].reshape(H * rows, F))
        dkv_acc[j, 1] += dot_nn(low, qall[s, 1].reshape(H * rows, F))

    def dkv_copy(k, b):
        return remote(dkv_send.at[k], dkv_recv.at[z], dkv_send_sem.at[k], dkv_recv_sem.at[z], me.at(z=b))

    def send_dq(g):
        for s in (2 * g, 2 * g + 1):
            for core in range(2):
                dq_send[s * 2 + core] = (dq_acc[s, :, core * T:(core + 1) * T] * scale).astype(BF16)
        for n in range(GROUP):
            p = GROUP * g + n

            @pl.when(p != i)
            def _():
                dq_copy(p).start()

    def dq_copy(p):
        return remote(dq_send.at[p], dq_recv.at[i], dq_send_sem.at[p], dq_recv_sem.at[i], me.at(i=p))

    near_pairs = (block_pairs + 1) // 2
    def second_step(m, carry):
        n = m - near_pairs
        j = jnp.where(n < 0, m, block_pairs - 1 - n)

        @pl.when(m == 0)
        def _():
            add_statistics(0)

        @pl.when(n == 0)
        def _():
            add_statistics(1)

        @pl.when(n == block_pairs - near_pairs)
        def _():
            send_dq(0)

        def over_chips(s, carry):
            second_unit(s, j)
            return carry

        first = jnp.where(n < 0, 0, jnp.where(j < near_pairs, 2, 0))
        lax.fori_loop(first, jnp.where(n < 0, 2, chips), over_chips, 0)

        @pl.when(n >= 0)
        def _():
            key_part = dot_nt(key_table, (dkv_acc[j, 0] * scale).astype(BF16)).astype(BF16)
            value_part = dot_nt(value_table, dkv_acc[j, 1].astype(BF16)).astype(BF16)
            for b in range(2):
                dkv_send[2 * j + b, 0:SK, :] = key_part[:, b * T:(b + 1) * T]
                dkv_send[2 * j + b, SK:, :] = value_part[:, b * T:(b + 1) * T]

        @pl.when(jnp.logical_and(n >= 0, 2 * j + 1 <= z))
        def _():
            dkv_copy(2 * j + 1, z - 2 * j - 1).start()

        @pl.when(jnp.logical_and(n >= 0, j > 0))
        def _():
            dkv_copy(2 * j, z - 2 * j).start()

        return carry

    lax.fori_loop(0, near_pairs + block_pairs, second_step, 0)
    send_dq(1)

    for copy in own_copies + ring_copies + list(sib_copies.values()) + iy_copies:
        copy.wait_send()
    if me.halves > 1:
        iz_copy.wait_send()

    for g in range(pairs):
        for copy in stat_copies(g):
            copy.wait_send()
    for p in range(width):
        @pl.when(p != i)
        def _():
            dq_copy(p).wait_send()

    def left_kv(n, carry):
        b = z - 2 * n

        for part in range(2):
            @pl.when(z + 2 < planes)
            def _():
                kv_copy(b, 2, part).wait_send()

            @pl.when(z + 1 < planes)
            def _():
                kv_copy(b, 1, part).wait_send()

        return carry

    lax.fori_loop(0, z // 2 + 1, left_kv, 0)

    def left_dkv(k, carry):
        dkv_copy(k, z - k).wait_send()
        return carry

    lax.fori_loop(1, z + 1, left_dkv, 0)

    if me.halves > 1:
        away = 1 - me.half
        remote(iz.at[away], iz.at[away], iz_send_sem.at[0], iz_recv_sem.at[away], me.at(half=away)).wait_recv()
    summed = iz[0].astype(F32)
    for half in range(1, me.halves):
        summed = summed + iz[half].astype(F32)
    input_sketch = summed * math.sqrt(SK / (x_ref.shape[1] * ys * halves))

    heads = me.ys * me.halves
    kv_factor = math.sqrt(SK / (F * heads))
    grad_sum[SK:3 * SK, :] = dkv_send[0].astype(F32) * kv_factor

    def add_kv(b, carry):
        remote(dkv_send.at[0], dkv_recv.at[b], dkv_send_sem.at[0], dkv_recv_sem.at[b], me.at(z=rem(z + 1, planes))).wait_recv()
        grad_sum[SK:3 * SK, :] += dkv_recv[b].astype(F32) * kv_factor
        return carry

    dq_recv[i] = dq_send[i]
    lax.fori_loop(z + 1, planes, add_kv, 0)
    for o in far_first(width):
        p = rem(i + o, width)
        remote(dq_send.at[p], dq_recv.at[p], dq_send_sem.at[0], dq_recv_sem.at[p], me.at(i=p)).wait_recv()
    query_sum = dq_recv[0].astype(F32)
    for p in range(1, width):
        query_sum = query_sum + dq_recv[p].astype(F32)
    grad_sum[0:SK, :] = query_sum * math.sqrt(SK / (H * F * heads))

    band = SK // ys
    masked = jnp.concatenate([jnp.where(doc_of == e, input_sketch, 0.0) for e in range(DOCS_MOST)], axis=0)
    grads = grad_sum[...]
    masked_high = masked.astype(BF16)
    masked_low = (masked - masked_high.astype(F32)).astype(BF16)
    grads_high = grads.astype(BF16)
    grads_low = (grads - grads_high.astype(F32)).astype(BF16)
    product = dot_nt(masked_high, grads_high) + (dot_nt(masked_high, grads_low) + dot_nt(masked_low, grads_high))
    product = product.reshape(DOCS_MOST // 2, 2, SK, 4 * SK)
    products[:, 0:2] = product[:, :, :, 0:2 * SK].astype(BF16)
    value_product = product[:, :, :, 2 * SK:]
    moved = pltpu.roll(value_product[:, 1].reshape(DOCS_MOST // 2 * SK, 2 * SK), SK, 1)
    products[:, 2] = (value_product[:, 0] + moved.reshape(DOCS_MOST // 2, SK, 2 * SK)).astype(BF16)

    def part(p, y):
        return products.at[p, :, pl.ds(pl.multiple_of(y * band, band), band), :]

    my_slot = place_in_group * ys + me.y
    near_copies = [
        remote(part(p, y), near.at[my_slot], pool.at[n], near_recv_sem.at[my_slot], me.at(i=group_first + p, y=y))
        for n, (p, y) in enumerate(near_peers)
    ]
    for copy in near_copies:
        copy.start()
    summed = part(place_in_group, me.y)[...].astype(F32)
    for p, y in near_peers:
        slot = p * ys + y
        remote(near.at[slot], near.at[slot], pool.at[0], near_recv_sem.at[slot], me.at(i=group_first + p, y=y)).wait_recv()
        summed = summed + near[slot].astype(F32)
    plane_docs[i] = summed.astype(BF16)

    plane_copies = [
        remote(plane_docs.at[i], plane_docs.at[i], dq_send_sem.at[o - 1], plane_recv_sem.at[i], me.at(i=rem(i + o, width)))
        for o in far_first(width)
    ]
    for copy in plane_copies:
        copy.start()
    for o in far_first(width):
        p = rem(i + o, width)
        remote(plane_docs.at[p], plane_docs.at[p], dq_send_sem.at[0], plane_recv_sem.at[p], me.at(i=p)).wait_recv()

    for copy in near_copies:
        copy.wait_send()

    my_line = z * halves + me.half
    own = band // halves

    def far_copy(fz, half):
        slot = fz * halves + half
        return remote(far_send.at[slot], far.at[my_line], pool.at[slot], far_recv_sem.at[my_line], me.at(z=fz, half=half))

    def gather_row(n, carry):
        fz = rem(z + n, planes)
        row = fz * width + i
        found = jnp.zeros((band, 2 * SK), F32)
        values = [jnp.zeros((band, 2 * SK), F32)] * 2
        for j in range(width):
            for e in range(2):
                chosen = doc_target[2 * j + e] == row
                found = found + jnp.where(chosen, plane_docs[j, e].astype(F32), 0.0)
                values[e] = values[e] + jnp.where(chosen, plane_docs[j, 2].astype(F32), 0.0)
        lanes = lax.broadcasted_iota(jnp.int32, (band, 2 * SK), 1)
        value_rows = jnp.where(lanes < SK, values[0] + pltpu.roll(values[1], SK, 1), 0.0)
        for half in range(halves):
            mine_of = slice(half * own, (half + 1) * own)
            both = jnp.concatenate([found[mine_of], value_rows[mine_of]], axis=0)
            far_send[fz * halves + half] = both.astype(BF16)

            @pl.when(jnp.logical_or(fz != z, me.half != half))
            def _():
                far_copy(fz, half).start()

        return carry

    lax.fori_loop(0, planes, gather_row, 0)
    for copy in plane_copies:
        copy.wait_send()
    result = far_send[my_line].astype(F32)
    for fz, half in far_peers:
        slot = fz * halves + half
        remote(far.at[slot], far.at[slot], pool.at[0], far_recv_sem.at[slot], me.at(z=fz, half=half)).wait_recv()
        result = result + far[slot].astype(F32)
    query_key, value_only = result[0:own], result[own:]
    key_query, moved_value = pltpu.roll(query_key, SK, 1), pltpu.roll(value_only, SK, 1)
    first_half = lax.broadcasted_iota(jnp.int32, (1, 2 * SK), 1) < SK
    for p, (even, odd) in enumerate(((query_key, key_query), (key_query, query_key), (value_only, moved_value))):
        for pair in range(own // 2):
            out_ref[0, p:p + 1, pair * 2 * SK:(pair + 1) * 2 * SK] = jnp.where(
                first_half, even[2 * pair:2 * pair + 1], odd[2 * pair + 1:2 * pair + 2]
            )
    for fz, half in far_peers:
        far_copy(fz, half).wait_send()


def sketches_of(
    doc_starts, doc_rows, layer_input, queries, key_states, value_states, out_grad,
    input_hash, query_hash, key_hash, value_hash,
):
    planes, chips, cores = SEQ_GRID
    ys, halves = HEAD_GRID
    width = chips * cores
    rows = 2 * T
    line = planes * halves
    band = SK // ys
    pairs = chips // 2
    dma = pltpu.SemaphoreType.DMA
    vmem = pltpu.VMEM
    return pl.pallas_call(
        kernel,
        out_shape=jax.ShapeDtypeStruct((1, 3, band // halves * SK), F32),
        in_specs=[pl.BlockSpec(memory_space=pl.ANY)] * 11,
        out_specs=pl.BlockSpec(memory_space=pltpu.VMEM),
        scratch_shapes=[
            vmem((chips, 2, H, rows, F), BF16),
            vmem((planes, 2, T, F), BF16),
            vmem((chips, planes // 2, 2 * T, H * rows), F32),
            vmem((chips, planes // 2, 2 * T, H * rows), F32),
            vmem((chips, 8, H * rows), F32),
            vmem((planes // 2, H * SK, 2 * T), BF16),
            vmem((pairs, 8, H * rows), F32),
            vmem((pairs, width, 8, H * rows), F32),
            vmem((chips, 8, H * rows), F32),
            vmem((chips, SK, rows), F32),
            vmem((planes // 2, 2, 2 * T, F), F32),
            vmem((planes, 2 * SK, T), BF16),
            vmem((planes, 2 * SK, T), BF16),
            vmem((width, SK, T), BF16),
            vmem((width, SK, T), BF16),
            vmem((ys, SK, T), BF16),
            vmem((halves, SK, T), BF16),
            vmem((4 * SK, T), F32),
            vmem((DOCS_MOST // 2, 3, SK, 2 * SK), BF16),
            vmem((GROUP * ys, 3, band, 2 * SK), BF16),
            vmem((width, 3, band, 2 * SK), BF16),
            vmem((2 * width, band, 2 * SK), jnp.int32),
            vmem((line, 2 * band // halves, 2 * SK), BF16),
            vmem((line, 2 * band // halves, 2 * SK), BF16),
            vmem(layer_input.shape, BF16),
            pltpu.SMEM(doc_starts.shape, jnp.int32), pltpu.SMEM(doc_rows.shape, jnp.int32),
            vmem(input_hash.shape, jnp.int32), vmem(query_hash.shape, jnp.int32),
            vmem(key_hash.shape, jnp.int32), vmem(value_hash.shape, jnp.int32),
            dma((2 + 2 * H + 7,)), pltpu.SemaphoreType.REGULAR((3,)),
            dma((chips, 2, 2)), dma((3, 2)), dma((2,)), dma((3, 2)),
            dma(((planes + 1) // 2, 2, 2)), dma((planes, 2)),
            dma((max(pairs * width, GROUP * ys, line),)), dma((pairs, width)),
            dma((planes,)), dma((planes,)),
            dma((width,)), dma((width,)),
            dma((ys,)), dma((ys,)), dma((halves,)), dma((halves,)),
            dma((GROUP * ys,)), dma((width,)), dma((line,)),
        ],
        compiler_params=pltpu.CompilerParams(
            collective_id=0, has_side_effects=True, vmem_limit_bytes=56 * 1024 * 1024
        ),
        name="sketches",
    )(
        doc_starts, doc_rows, layer_input, queries, key_states, value_states, out_grad,
        input_hash, query_hash, key_hash, value_hash,
    )


def on_device(
    layer_input, queries, key_states, value_states, out_grad,
    input_hash, query_hash, key_hash, value_hash, doc_starts, doc_rows,
):
    return sketches_of(
        doc_starts, doc_rows, layer_input, queries, key_states, value_states, out_grad,
        input_hash, query_hash, key_hash, value_hash,
    )


def solution(mesh):
    return jax.shard_map(
        on_device,
        mesh=mesh,
        in_specs=(
            P("seq", "head"), P("seq", "head"), P("seq", "head"), P("seq", "head"), P("seq", "head"),
            P(None, "head"), P(None, "head"), P(None, "head"), P(None, "head"),
            P(), P(),
        ),
        out_specs=P("seq", None, "head"),
        check_vma=False,
    )
```

```python
import functools
import math

import jax
import jax.numpy as jnp
from jax import lax
from jax.experimental import pallas as pl
from jax.experimental.pallas import tpu as pltpu
from jax.sharding import PartitionSpec as P

SEQ_GRID = (8, 4, 2)
HEAD_GRID = (4, 2)

T = 128
F = 128
H = 4
SK = 64
GROUP = 4
DOCS_MOST = 8
LOW = -1e30
MESH = pl.DeviceIdType.MESH
F32 = jnp.float32
BF16 = jnp.bfloat16


def dot_nt(a, b):
    return lax.dot_general(a, b, (((1,), (1,)), ((), ())), preferred_element_type=F32)


def dot_nn(a, b):
    return jnp.dot(a, b, preferred_element_type=F32)


def sign_table(hashes):
    buckets = lax.broadcasted_iota(jnp.int32, (SK, hashes.shape[1]), 0)
    signs = (1 - 2 * (hashes[1:2, :] & 1)).astype(F32)
    return jnp.where(buckets == hashes[0:1, :], signs, 0.0).astype(BF16)


def rem(value, count):
    return lax.rem(value + count, count)


def far_first(count):
    return sorted(range(1, count), key=lambda o: -min(o, count - o))


class Place:
    def __init__(self):
        self.planes, self.chips, self.cores = SEQ_GRID
        self.ys, self.halves = HEAD_GRID
        self.width = self.chips * self.cores
        seq = lax.axis_index("seq")
        head = lax.axis_index("head")
        self.seq, self.head = seq, head
        self.i = lax.rem(seq, self.width)
        self.z = seq // self.width
        self.c = lax.rem(self.i, self.cores)
        self.x = self.i // self.cores
        self.y = head // self.halves
        self.half = lax.rem(head, self.halves)

    def at(self, z=None, i=None, y=None, half=None):
        z = self.z if z is None else z
        i = self.i if i is None else i
        y = self.y if y is None else y
        half = self.half if half is None else half
        return (z * self.width + i, y * self.halves + half)


def remote(src, dst, send_sem, recv_sem, device):
    return pltpu.make_async_remote_copy(
        src_ref=src, dst_ref=dst, send_sem=send_sem, recv_sem=recv_sem, device_id=device, device_id_type=MESH
    )


def greet(devices):
    barrier = pltpu.get_barrier_semaphore()
    for device in devices:
        pl.semaphore_signal(barrier, inc=1, device_id=device, device_id_type=MESH)


def kernel(
    starts_ref, targets_ref, x_ref, q_ref, k_ref, v_ref, do_ref, xh_ref, qh_ref, kh_ref, vh_ref,
    out_ref,
    qall, kv, scores, wgrads, stat, kmt, stat_send, stat_recv, total, dq_acc, dkv_acc,
    dkv_send, dkv_recv, dkv_up, dq_send, dq_recv, iy, iz, grad_sum,
    products, near, plane_docs, doc_target, far_send, far,
    inputs, starts, targets, input_hash, query_hash, key_hash, value_hash, input_sem, hello, q_recv, q_own, q_ring, q_sib, kv_send_sem, kv_recv_sem, pool, st_recv_sem,
    dkv_send_sem, dkv_recv_sem, up_recv_sem, dq_send_sem, dq_recv_sem, iy_send_sem, iy_recv_sem, iz_send_sem, iz_recv_sem,
    near_recv_sem, plane_recv_sem, far_recv_sem,
):
    me = Place()
    planes, chips, width = me.planes, me.chips, me.width
    x, c, z, i = me.x, me.c, me.z, me.i
    rows = 2 * T
    scale = 1.0 / math.sqrt(F)
    scale2 = scale * math.log2(math.e)

    ys, halves = me.ys, me.halves
    place_in_group = lax.rem(i, GROUP)
    group_first = i - place_in_group
    near_peers = []
    for p in far_first(GROUP) + [0]:
        for y in far_first(ys) + [0]:
            if (p, y) != (0, 0):
                near_peers.append((rem(place_in_group + p, GROUP), rem(me.y + y, ys)))
    far_peers = []
    for o in range(1, planes * halves):
        far_peers.append((rem(z + o // halves, planes), rem(me.half + o % halves, halves)))
    line = planes * halves

    def along(steps):
        to = rem(me.half * planes + z + steps, line)
        return me.at(z=lax.rem(to, planes), half=to // planes)

    friends = [along(o) for o in sorted({o % line for o in (1, 2, -1, -2)} - {0})]
    hellos = 3 if line > 5 else 0

    def pass_hello(n):
        for steps in (2, -2):
            pl.semaphore_signal(hello.at[n], inc=1, device_id=along(steps), device_id_type=MESH)

    def hear_hello(n):
        pl.semaphore_wait(hello.at[n], 2)

    friends += [me.at(y=rem(me.y + o, ys)) for o in range(1, ys)]
    friends += [me.at(i=rem(i + o, width)) for o in far_first(width)]
    greet(friends)

    mine = pl.ds(pl.multiple_of(c * T, T), T)
    loads = [pltpu.make_async_copy(k_ref, kv.at[z, 0], input_sem.at[0]), pltpu.make_async_copy(v_ref, kv.at[z, 1], input_sem.at[1])]
    for part, ref in enumerate((q_ref, do_ref)):
        for h in range(H):
            loads.append(
                pltpu.make_async_copy(
                    ref.at[:, pl.ds(h * F, F)], qall.at[x, part, h, mine, :], input_sem.at[2 + part * H + h]
                )
            )
    later = (
        (x_ref, inputs), (xh_ref, input_hash), (qh_ref, query_hash), (kh_ref, key_hash), (vh_ref, value_hash),
        (starts_ref, starts), (targets_ref, targets),
    )
    later_loads = [
        pltpu.make_async_copy(ref, place, input_sem.at[2 + 2 * H + n]) for n, (ref, place) in enumerate(later)
    ]
    for load in loads + later_loads:
        load.start()
    for load in loads:
        load.wait()

    def piece(step, core, part):
        s = rem(x + step, chips)
        ref = qall.at[s, part, :, pl.ds(pl.multiple_of(core * T, T), T), :]
        return ref, q_recv.at[s, core, part]

    def send_piece(step, core, part, send_sem, target):
        ref, recv_sem = piece(step, core, part)
        return remote(ref, ref, send_sem, recv_sem, target)

    sibling = me.at(i=x * 2 + 1 - c)
    right = me.at(i=rem(x + 1, chips) * 2 + c)
    left = me.at(i=rem(x + chips - 1, chips) * 2 + c)
    own_copies = [
        send_piece(0, c, part, q_own.at[n, part], target)
        for n, target in enumerate((sibling, right, left)) for part in range(2)
    ]
    ring_copies = [
        send_piece(chips - 1, c, 0, q_ring.at[0], right),
        send_piece(1, c, 1, q_ring.at[1], left),
    ]
    sib_copies = {
        (step, part): send_piece(step, c, part, q_sib.at[step - 1, part], sibling)
        for step in (1, 2, 3) for part in range(2)
    }

    def wait_piece(step, core, part):
        ref, recv_sem = piece(step, core, part)
        remote(ref, ref, q_own.at[0, 0], recv_sem, sibling).wait_recv()

    def kv_copy(b, hops, part):
        return remote(
            kv.at[b, part], kv.at[b, part], kv_send_sem.at[b // 2, hops - 1, part], kv_recv_sem.at[b, part],
            me.at(z=rem(z + hops, planes)),
        )

    def relay_kv(b, part):
        @pl.when(z + 2 < planes)
        def _():
            kv_copy(b, 2, part).start()

        @pl.when(z + 1 < planes)
        def _():
            kv_copy(b, 1, part).start()

    pl.semaphore_wait(pltpu.get_barrier_semaphore(), len(friends))

    for part in range(2):
        relay_kv(z, part)
    for target, part in ((1, 0), (2, 1), (0, 0), (0, 1), (1, 1), (2, 0)):
        own_copies[2 * target + part].start()

    if hellos:
        pass_hello(0)
    for load in later_loads:
        load.wait()

    input_part = dot_nt(sign_table(input_hash[...]), inputs[...])
    iy[me.y] = input_part.astype(BF16)
    query_table = sign_table(query_hash[...])
    query_tables = jnp.concatenate([query_table[:, h * F:(h + 1) * F] for h in range(H)], axis=0)
    key_table = sign_table(key_hash[...])
    value_table = sign_table(value_hash[...])
    for s in range(chips):
        stat[s, 0:1, :] = jnp.full((1, H * rows), LOW, F32)
        stat[s, 1:3, :] = jnp.zeros((2, H * rows), F32)
    dq_acc[...] = jnp.zeros_like(dq_acc)
    dkv_acc[...] = jnp.zeros_like(dkv_acc)
    grad_sum[3 * SK:, :] = jnp.zeros((SK, T), F32)

    doc_count = starts.shape[0]
    group_tokens = GROUP * T
    tokens = lax.broadcasted_iota(jnp.int32, (1, T), 1)
    here = tokens + me.seq * T
    here_group = (me.seq // GROUP) * group_tokens
    slot_group = (z * (width // GROUP) + tokens // (2 * GROUP)) * group_tokens
    doc_of = jnp.zeros((1, T), jnp.int32)
    slot_first = jnp.zeros((1, T), jnp.int32)
    slot_past = jnp.zeros((1, T), jnp.int32)
    for d in range(doc_count):
        begins = starts[d]
        doc_of = doc_of + jnp.where(jnp.logical_and(begins <= here, begins > here_group), 1, 0)
        slot_first = slot_first + jnp.where(begins < slot_group, 1, 0)
        slot_past = slot_past + jnp.where(begins < slot_group + group_tokens, 1, 0)
    slot_doc = slot_first + lax.rem(tokens, 2 * GROUP)
    slot_doc = jnp.where(slot_doc < slot_past, slot_doc, -1)
    slot_row = jnp.full((1, T), -1, jnp.int32)
    for d in range(doc_count):
        slot_row = jnp.where(slot_doc == d, targets[d], slot_row)
    for n in range(2 * width):
        doc_target[n] = jnp.broadcast_to(slot_row[:, n:n + 1], doc_target.shape[1:])

    iy_copies = [
        remote(iy.at[me.y], iy.at[me.y], iy_send_sem.at[o - 1], iy_recv_sem.at[me.y], me.at(y=rem(me.y + o, me.ys)))
        for o in range(1, me.ys)
    ]
    for copy in iy_copies:
        copy.start()
    iz_copy = remote(iz.at[me.half], iz.at[me.half], iz_send_sem.at[0], iz_recv_sem.at[me.half], me.at(half=1 - me.half))

    def input_over_y():
        for o in range(1, me.ys):
            y = rem(me.y + o, me.ys)
            remote(iy.at[y], iy.at[y], iy_send_sem.at[0], iy_recv_sem.at[y], me.at(y=y)).wait_recv()
        summed = iy[0].astype(F32)
        for y in range(1, me.ys):
            summed = summed + iy[y].astype(F32)
        iz[me.half] = summed.astype(BF16)

    block_pairs = z // 2 + 1

    def two_blocks(j, part):
        return jnp.concatenate([kv[z - 2 * j, part], kv[jnp.maximum(z - 2 * j - 1, 0), part]], axis=0)

    def first_unit(s, j, masked):
        keys, values = two_blocks(j, 0), two_blocks(j, 1)
        for h in range(H):
            cols = pl.ds(h * rows, rows)
            st = dot_nt(keys, qall[s, 0, h]) * scale2
            if masked:
                row = lax.broadcasted_iota(jnp.int32, (2 * T, rows), 0)
                near_place = jnp.where(j == 0, i * T, -T)
                far_place = jnp.where(2 * j + 1 <= z, -2 * T, rows * chips)
                query_place = lax.broadcasted_iota(jnp.int32, (2 * T, rows), 1) + s * rows
                st = jnp.where(row + jnp.where(row < T, near_place, far_place) <= query_place, st, LOW)
            dp = dot_nt(values, qall[s, 1, h])
            scores[s, j, :, cols] = st
            wgrads[s, j, :, cols] = dp
            old_top = stat[s, 0:1, cols]
            top = jnp.maximum(old_top, jnp.max(st, axis=0, keepdims=True))
            e = jnp.exp2(st - top)
            keep = jnp.exp2(old_top - top)
            stat[s, 0:1, cols] = top
            stat[s, 1:2, cols] = stat[s, 1:2, cols] * keep + jnp.sum(e, axis=0, keepdims=True)
            stat[s, 2:3, cols] = stat[s, 2:3, cols] * keep + jnp.sum(e * dp, axis=0, keepdims=True)

    def arrived_kv(t):
        for part in range(2):
            kv_copy(z - t, 1, part).wait_recv()

    def sketch_keys(j):
        kmt[j] = dot_nt(query_tables, two_blocks(j, 0)).astype(BF16)

    def first_blocks(s, low, high):
        def over_blocks(j, carry):
            bordering = jnp.logical_or(j == 0, 2 * j == z)

            @pl.when(bordering)
            def _():
                first_unit(s, j, True)

            @pl.when(jnp.logical_not(bordering))
            def _():
                first_unit(s, j, False)

            return carry

        lax.fori_loop(low, high, over_blocks, 0)

    def even_arrival(t):
        @pl.when(t <= z)
        def _():
            for part in range(2):
                kv_copy(z - t, 1, part).wait_recv()
                relay_kv(z - t, part)

    def odd_arrival(t):
        @pl.when(t <= z)
        def _():
            arrived_kv(t)

        @pl.when(t // 2 < block_pairs)
        def _():
            sketch_keys(t // 2)

    def hand_on(step, part):
        wait_piece(step, c, part)
        sib_copies[(step, part)].start()

    pairs = chips // 2

    def stat_copies(g):
        return [
            remote(
                stat_send.at[g], stat_recv.at[g, i], pool.at[g * width + o - 1], st_recv_sem.at[g, i],
                me.at(i=rem(i + o, width)),
            )
            for o in far_first(width)
        ]

    def first_step(n, carry):
        @pl.when(n == 0)
        def _():
            even_arrival(2)
            for n, (step, part) in enumerate(((chips - 1, 0), (1, 1))):
                wait_piece(step, c, part)
                ring_copies[n].start()
                sib_copies[(step, part)].start()
            odd_arrival(1)
            for part in range(2):
                wait_piece(0, 1 - c, part)

        @pl.when(n == 1)
        def _():
            even_arrival(4)
            hand_on(chips - 1, 1)
            hand_on(1, 0)
            if hellos:
                hear_hello(0)
                pass_hello(1)
            odd_arrival(3)

        @pl.when(n == 2)
        def _():
            for step in (chips - 1, 1):
                for part in range(2):
                    wait_piece(step, 1 - c, part)
            input_over_y()

        @pl.when(n == 3)
        def _():
            hand_on(2, 0)
            hand_on(2, 1)
            even_arrival(6)
            if hellos:
                hear_hello(1)
                pass_hello(2)

        @pl.when(n == 4)
        def _():
            odd_arrival(5)

        @pl.when(n == 7)
        def _():
            odd_arrival(7)
            for part in range(2):
                wait_piece(2, 1 - c, part)

        s = jnp.where(n < 2, x, jnp.where(n == 2, x + 1, jnp.where(n == 3, x + chips - 1, x + n - 5)))
        s = jnp.where(n < 7, rem(s, chips), n - 7)
        low = jnp.where(n < 2, n, jnp.where(n < 4, 0, jnp.where(n < 7, 2, jnp.where(s == rem(x + 2, chips), 0, 3))))
        high = jnp.where(n < 2, n + 1, jnp.where(n < 4, 2, jnp.where(n < 7, 3, 4)))
        first_blocks(s, low, jnp.minimum(high, block_pairs))

        @pl.when(jnp.logical_or(n == 8, n == 10))
        def _():
            g = (n - 8) // 2
            for m in range(2):
                stat_send[g, 3 * m:3 * m + 3, :] = stat[2 * g + m, 0:3, :]
            for copy in stat_copies(g):
                copy.start()
            stat_recv[g, i] = stat_send[g]

        return carry

    lax.fori_loop(0, 11, first_step, 0)
    if hellos:
        hear_hello(2)
    if me.halves > 1:
        iz_copy.start()

    def add_statistics(g):
        for o in far_first(width):
            p = rem(i + o, width)
            remote(
                stat_send.at[g], stat_recv.at[g, p], pool.at[0], st_recv_sem.at[g, p], me.at(i=p)
            ).wait_recv()
        for n in range(2):
            first = 3 * n
            top = stat_recv[g, 0, first:first + 1, :]
            for p in range(1, width):
                top = jnp.maximum(top, stat_recv[g, p, first:first + 1, :])
            weight_sum = jnp.zeros_like(top)
            delta_sum = jnp.zeros_like(top)
            for p in range(width):
                factor = jnp.exp2(stat_recv[g, p, first:first + 1, :] - top)
                weight_sum = weight_sum + stat_recv[g, p, first + 1:first + 2, :] * factor
                delta_sum = delta_sum + stat_recv[g, p, first + 2:first + 3, :] * factor
            total[2 * g + n, 0:1, :] = top + jnp.log2(weight_sum)
            total[2 * g + n, 1:2, :] = delta_sum / weight_sum

    def second_unit(s, j):
        lows, grads = [], []
        for h in range(H):
            cols = pl.ds(h * rows, rows)
            p = jnp.exp2(scores[s, j, :, cols] - total[s, 0:1, cols])
            g = p * (wgrads[s, j, :, cols] - total[s, 1:2, cols])
            lows.append(p.astype(BF16))
            g = g.astype(BF16)
            grads.append(g)
            dq_acc[s] += dot_nn(kmt[j, h * SK:(h + 1) * SK, :], g)
        low = jnp.concatenate(lows, axis=1)
        grad = jnp.concatenate(grads, axis=1)
        dkv_acc[j, 0] += dot_nn(grad, qall[s, 0].reshape(H * rows, F))
        dkv_acc[j, 1] += dot_nn(low, qall[s, 1].reshape(H * rows, F))

    odd_plane = lax.rem(z, 2) == 1
    even_plane = lax.rem(z, 2) == 0

    def hand_down(k):
        return remote(
            dkv_send.at[k], dkv_up.at[z - k], dkv_send_sem.at[k], up_recv_sem.at[z - k], me.at(z=rem(z - 1, planes))
        )

    def dkv_copy(k, b):
        return remote(
            dkv_send.at[k], dkv_recv.at[z // 2], dkv_send_sem.at[k], dkv_recv_sem.at[z // 2], me.at(z=b)
        )

    def add_and_send(j):
        for k in (2 * j + 1, 2 * j):
            @pl.when(k <= z)
            def _():
                b = z - k
                remote(
                    dkv_send.at[0], dkv_up.at[b], dkv_send_sem.at[0], up_recv_sem.at[b], me.at(z=rem(z + 1, planes))
                ).wait_recv()
                dkv_send[k] = (dkv_send[k].astype(F32) + dkv_up[b].astype(F32)).astype(BF16)

                @pl.when(k > 0)
                def _():
                    dkv_copy(k, b).start()

    def send_dq(g):
        for s in (2 * g, 2 * g + 1):
            for core in range(2):
                dq_send[s * 2 + core] = (dq_acc[s, :, core * T:(core + 1) * T] * scale).astype(BF16)
        for n in range(GROUP):
            p = GROUP * g + n

            @pl.when(p != i)
            def _():
                dq_copy(p).start()

    def dq_copy(p):
        return remote(dq_send.at[p], dq_recv.at[i], dq_send_sem.at[p], dq_recv_sem.at[i], me.at(i=p))

    near_pairs = (block_pairs + 1) // 2
    def second_step(m, carry):
        n = m - near_pairs
        j = jnp.where(n < 0, m, block_pairs - 1 - n)

        @pl.when(m == 0)
        def _():
            add_statistics(0)

        @pl.when(n == 0)
        def _():
            add_statistics(1)

        @pl.when(n == block_pairs - near_pairs)
        def _():
            send_dq(0)

        def over_chips(s, carry):
            second_unit(s, j)
            return carry

        first = jnp.where(n < 0, 0, jnp.where(j < near_pairs, 2, 0))
        lax.fori_loop(first, jnp.where(n < 0, 2, chips), over_chips, 0)

        @pl.when(n >= 0)
        def _():
            key_part = dot_nt(key_table, (dkv_acc[j, 0] * scale).astype(BF16)).astype(BF16)
            value_part = dot_nt(value_table, dkv_acc[j, 1].astype(BF16)).astype(BF16)
            for b in range(2):
                dkv_send[2 * j + b, 0:SK, :] = key_part[:, b * T:(b + 1) * T]
                dkv_send[2 * j + b, SK:, :] = value_part[:, b * T:(b + 1) * T]

        @pl.when(jnp.logical_and(n >= 0, odd_plane))
        def _():
            hand_down(2 * j + 1).start()

        @pl.when(jnp.logical_and(n >= 0, jnp.logical_and(odd_plane, j > 0)))
        def _():
            hand_down(2 * j).start()

        @pl.when(jnp.logical_and(n >= 1, even_plane))
        def _():
            add_and_send(j + 1)

        return carry

    lax.fori_loop(0, near_pairs + block_pairs, second_step, 0)
    send_dq(1)

    @pl.when(even_plane)
    def _():
        add_and_send(0)

    for copy in own_copies + ring_copies + list(sib_copies.values()) + iy_copies:
        copy.wait_send()
    if me.halves > 1:
        iz_copy.wait_send()

    for g in range(pairs):
        for copy in stat_copies(g):
            copy.wait_send()
    for p in range(width):
        @pl.when(p != i)
        def _():
            dq_copy(p).wait_send()

    def left_kv(n, carry):
        b = z - 2 * n

        for part in range(2):
            @pl.when(z + 2 < planes)
            def _():
                kv_copy(b, 2, part).wait_send()

            @pl.when(z + 1 < planes)
            def _():
                kv_copy(b, 1, part).wait_send()

        return carry

    lax.fori_loop(0, z // 2 + 1, left_kv, 0)

    def left_dkv(k, carry):
        dkv_copy(k, z - k).wait_send()
        return carry

    lax.fori_loop(1, z + 1, left_dkv, 0)

    if me.halves > 1:
        away = 1 - me.half
        remote(iz.at[away], iz.at[away], iz_send_sem.at[0], iz_recv_sem.at[away], me.at(half=away)).wait_recv()
    summed = iz[0].astype(F32)
    for half in range(1, me.halves):
        summed = summed + iz[half].astype(F32)
    input_sketch = summed * math.sqrt(SK / (x_ref.shape[1] * ys * halves))

    heads = me.ys * me.halves
    kv_factor = math.sqrt(SK / (F * heads))
    grad_sum[SK:3 * SK, :] = dkv_send[0].astype(F32) * kv_factor

    def add_kv(m, carry):
        remote(
            dkv_send.at[0], dkv_recv.at[m], dkv_send_sem.at[0], dkv_recv_sem.at[m], me.at(z=rem(z + 1, planes))
        ).wait_recv()
        grad_sum[SK:3 * SK, :] += dkv_recv[m].astype(F32) * kv_factor
        return carry

    dq_recv[i] = dq_send[i]
    lax.fori_loop(z // 2 + 1, planes // 2, add_kv, 0)
    for o in far_first(width):
        p = rem(i + o, width)
        remote(dq_send.at[p], dq_recv.at[p], dq_send_sem.at[0], dq_recv_sem.at[p], me.at(i=p)).wait_recv()
    query_sum = dq_recv[0].astype(F32)
    for p in range(1, width):
        query_sum = query_sum + dq_recv[p].astype(F32)
    grad_sum[0:SK, :] = query_sum * math.sqrt(SK / (H * F * heads))

    band = SK // ys
    masked = jnp.concatenate([jnp.where(doc_of == e, input_sketch, 0.0) for e in range(DOCS_MOST)], axis=0)
    grads = grad_sum[...]
    masked_high = masked.astype(BF16)
    masked_low = (masked - masked_high.astype(F32)).astype(BF16)
    grads_high = grads.astype(BF16)
    grads_low = (grads - grads_high.astype(F32)).astype(BF16)
    product = dot_nt(masked_high, grads_high) + (dot_nt(masked_high, grads_low) + dot_nt(masked_low, grads_high))
    product = product.reshape(DOCS_MOST // 2, 2, SK, 4 * SK)
    products[:, 0:2] = product[:, :, :, 0:2 * SK].astype(BF16)
    value_product = product[:, :, :, 2 * SK:]
    moved = pltpu.roll(value_product[:, 1].reshape(DOCS_MOST // 2 * SK, 2 * SK), SK, 1)
    products[:, 2] = (value_product[:, 0] + moved.reshape(DOCS_MOST // 2, SK, 2 * SK)).astype(BF16)

    def part(p, y):
        return products.at[p, :, pl.ds(pl.multiple_of(y * band, band), band), :]

    my_slot = place_in_group * ys + me.y
    near_copies = [
        remote(part(p, y), near.at[my_slot], pool.at[n], near_recv_sem.at[my_slot], me.at(i=group_first + p, y=y))
        for n, (p, y) in enumerate(near_peers)
    ]
    for copy in near_copies:
        copy.start()
    summed = part(place_in_group, me.y)[...].astype(F32)
    for p, y in near_peers:
        slot = p * ys + y
        remote(near.at[slot], near.at[slot], pool.at[0], near_recv_sem.at[slot], me.at(i=group_first + p, y=y)).wait_recv()
        summed = summed + near[slot].astype(F32)
    plane_docs[i] = summed.astype(BF16)

    plane_copies = [
        remote(plane_docs.at[i], plane_docs.at[i], dq_send_sem.at[o - 1], plane_recv_sem.at[i], me.at(i=rem(i + o, width)))
        for o in far_first(width)
    ]
    for copy in plane_copies:
        copy.start()
    for o in far_first(width):
        p = rem(i + o, width)
        remote(plane_docs.at[p], plane_docs.at[p], dq_send_sem.at[0], plane_recv_sem.at[p], me.at(i=p)).wait_recv()

    for copy in near_copies:
        copy.wait_send()

    my_line = z * halves + me.half
    own = band // halves

    def far_copy(fz, half):
        slot = fz * halves + half
        return remote(far_send.at[slot], far.at[my_line], pool.at[slot], far_recv_sem.at[my_line], me.at(z=fz, half=half))

    def gather_row(n, carry):
        fz = rem(z + n, planes)
        row = fz * width + i
        found = jnp.zeros((band, 2 * SK), F32)
        values = [jnp.zeros((band, 2 * SK), F32)] * 2
        for j in range(width):
            for e in range(2):
                chosen = doc_target[2 * j + e] == row
                found = found + jnp.where(chosen, plane_docs[j, e].astype(F32), 0.0)
                values[e] = values[e] + jnp.where(chosen, plane_docs[j, 2].astype(F32), 0.0)
        lanes = lax.broadcasted_iota(jnp.int32, (band, 2 * SK), 1)
        value_rows = jnp.where(lanes < SK, values[0] + pltpu.roll(values[1], SK, 1), 0.0)
        for half in range(halves):
            mine_of = slice(half * own, (half + 1) * own)
            both = jnp.concatenate([found[mine_of], value_rows[mine_of]], axis=0)
            far_send[fz * halves + half] = both.astype(BF16)

            @pl.when(jnp.logical_or(fz != z, me.half != half))
            def _():
                far_copy(fz, half).start()

        return carry

    lax.fori_loop(0, planes, gather_row, 0)
    for copy in plane_copies:
        copy.wait_send()
    result = far_send[my_line].astype(F32)
    for fz, half in far_peers:
        slot = fz * halves + half
        remote(far.at[slot], far.at[slot], pool.at[0], far_recv_sem.at[slot], me.at(z=fz, half=half)).wait_recv()
        result = result + far[slot].astype(F32)
    query_key, value_only = result[0:own], result[own:]
    key_query, moved_value = pltpu.roll(query_key, SK, 1), pltpu.roll(value_only, SK, 1)
    first_half = lax.broadcasted_iota(jnp.int32, (1, 2 * SK), 1) < SK
    for p, (even, odd) in enumerate(((query_key, key_query), (key_query, query_key), (value_only, moved_value))):
        for pair in range(own // 2):
            out_ref[0, p:p + 1, pair * 2 * SK:(pair + 1) * 2 * SK] = jnp.where(
                first_half, even[2 * pair:2 * pair + 1], odd[2 * pair + 1:2 * pair + 2]
            )
    for fz, half in far_peers:
        far_copy(fz, half).wait_send()


def sketches_of(
    doc_starts, doc_rows, layer_input, queries, key_states, value_states, out_grad,
    input_hash, query_hash, key_hash, value_hash,
):
    planes, chips, cores = SEQ_GRID
    ys, halves = HEAD_GRID
    width = chips * cores
    rows = 2 * T
    line = planes * halves
    band = SK // ys
    pairs = chips // 2
    dma = pltpu.SemaphoreType.DMA
    vmem = pltpu.VMEM
    return pl.pallas_call(
        kernel,
        out_shape=jax.ShapeDtypeStruct((1, 3, band // halves * SK), F32),
        in_specs=[pl.BlockSpec(memory_space=pl.ANY)] * 11,
        out_specs=pl.BlockSpec(memory_space=pltpu.VMEM),
        scratch_shapes=[
            vmem((chips, 2, H, rows, F), BF16),
            vmem((planes, 2, T, F), BF16),
            vmem((chips, planes // 2, 2 * T, H * rows), F32),
            vmem((chips, planes // 2, 2 * T, H * rows), F32),
            vmem((chips, 8, H * rows), F32),
            vmem((planes // 2, H * SK, 2 * T), BF16),
            vmem((pairs, 8, H * rows), F32),
            vmem((pairs, width, 8, H * rows), F32),
            vmem((chips, 8, H * rows), F32),
            vmem((chips, SK, rows), F32),
            vmem((planes // 2, 2, 2 * T, F), F32),
            vmem((planes, 2 * SK, T), BF16),
            vmem((planes // 2, 2 * SK, T), BF16),
            vmem((planes, 2 * SK, T), BF16),
            vmem((width, SK, T), BF16),
            vmem((width, SK, T), BF16),
            vmem((ys, SK, T), BF16),
            vmem((halves, SK, T), BF16),
            vmem((4 * SK, T), F32),
            vmem((DOCS_MOST // 2, 3, SK, 2 * SK), BF16),
            vmem((GROUP * ys, 3, band, 2 * SK), BF16),
            vmem((width, 3, band, 2 * SK), BF16),
            vmem((2 * width, band, 2 * SK), jnp.int32),
            vmem((line, 2 * band // halves, 2 * SK), BF16),
            vmem((line, 2 * band // halves, 2 * SK), BF16),
            vmem(layer_input.shape, BF16),
            pltpu.SMEM(doc_starts.shape, jnp.int32), pltpu.SMEM(doc_rows.shape, jnp.int32),
            vmem(input_hash.shape, jnp.int32), vmem(query_hash.shape, jnp.int32),
            vmem(key_hash.shape, jnp.int32), vmem(value_hash.shape, jnp.int32),
            dma((2 + 2 * H + 7,)), pltpu.SemaphoreType.REGULAR((3,)),
            dma((chips, 2, 2)), dma((3, 2)), dma((2,)), dma((3, 2)),
            dma(((planes + 1) // 2, 2, 2)), dma((planes, 2)),
            dma((max(pairs * width, GROUP * ys, line),)), dma((pairs, width)),
            dma((planes,)), dma((planes // 2,)), dma((planes,)),
            dma((width,)), dma((width,)),
            dma((ys,)), dma((ys,)), dma((halves,)), dma((halves,)),
            dma((GROUP * ys,)), dma((width,)), dma((line,)),
        ],
        compiler_params=pltpu.CompilerParams(
            collective_id=0, has_side_effects=True, vmem_limit_bytes=56 * 1024 * 1024
        ),
        name="sketches",
    )(
        doc_starts, doc_rows, layer_input, queries, key_states, value_states, out_grad,
        input_hash, query_hash, key_hash, value_hash,
    )


def on_device(
    layer_input, queries, key_states, value_states, out_grad,
    input_hash, query_hash, key_hash, value_hash, doc_starts, doc_rows,
):
    return sketches_of(
        doc_starts, doc_rows, layer_input, queries, key_states, value_states, out_grad,
        input_hash, query_hash, key_hash, value_hash,
    )


def solution(mesh):
    return jax.shard_map(
        on_device,
        mesh=mesh,
        in_specs=(
            P("seq", "head"), P("seq", "head"), P("seq", "head"), P("seq", "head"), P("seq", "head"),
            P(None, "head"), P(None, "head"), P(None, "head"), P(None, "head"),
            P(), P(),
        ),
        out_specs=P("seq", None, "head"),
        check_vma=False,
    )
```
